512 devices in a mesh: ctx: 64 (over x, z, core), head: 8 (over y).
Axes of the slice: x: 4, y: 8, z: 8, core: 2. Of those that a mesh axis runs over, the one named last changes fastest.
Arguments:
- lin_query: bfloat16 [8192, 32, 128], P('ctx', 'head'), may hold values from -6 to 6
- lin_keys: bfloat16 [8192, 32, 128], P('ctx', 'head'), may hold values from -1.5 to 1.5
- lin_values: bfloat16 [8192, 32, 128], P('ctx', 'head'), may hold values from -6 to 6
- log_decay: float32 [32, 8192], P('head', 'ctx'), may hold values from -1 to 0
- norm_gain: float32 [32, 128], P('head'), may hold values from 0.1 to 1.9
- lin_cotangent: bfloat16 [8192, 32, 128], P('ctx', 'head'), may hold values from -6 to 6
- soft_query: bfloat16 [8192, 32, 128], P('ctx', 'head'), may hold values from -6 to 6
- soft_keys: bfloat16 [8192, 32, 128], P('ctx', 'head'), may hold values from -6 to 6
- soft_values: bfloat16 [8192, 32, 128], P('ctx', 'head'), may hold values from -6 to 6
- soft_cotangent: bfloat16 [8192, 32, 128], P('ctx', 'head'), may hold values from -6 to 6
- doc_start: int32 [8192], P('ctx'), may hold values from 0 to 8191, as said below
Outputs:
- lin_output: bfloat16 [8192, 32, 128], P('ctx', 'head')
- lin_query_grad: bfloat16 [8192, 32, 128], P('ctx', 'head')
- lin_key_grad: bfloat16 [8192, 32, 128], P('ctx', 'head')
- lin_value_grad: bfloat16 [8192, 32, 128], P('ctx', 'head')
- soft_output: bfloat16 [8192, 32, 128], P('ctx', 'head')
- soft_query_grad: bfloat16 [8192, 32, 128], P('ctx', 'head')
- soft_key_grad: bfloat16 [8192, 32, 128], P('ctx', 'head')
- soft_value_grad: bfloat16 [8192, 32, 128], P('ctx', 'head')
The draws below stay inside these ranges and needn't reach their ends.
Inputs may be any that keep to these rules, and one draw needn't show every extreme that they name: doc_start[t] is where token t's document begins: it never falls, equals t or doc_start[t - 1], and t - doc_start[t] < 512; every draw holds a document of exactly 512 tokens, and the last token begins a document of its own.
All inputs are finite; a program needn't handle non-finite values.
Results may differ from the reference program's by a relative error of at most 0.03.
Values may be sent and summed in bfloat16 or wider, within the bound.
A program may use at most 128 MiB of HBM per device.

```python
import math
import jax
import jax.numpy as jnp
from jax import lax

DH = 128
TOK_DEV = 128
SPAN = 4
ATTENTION_GROUPS = 32
SEQUENCE_ENTRIES = 8192
N_CTX = 64


def draw_log_decay(key, part):
    key = jax.random.fold_in(key, 3)
    maximal_segment = SPAN * TOK_DEV
    slowest = 0.5 / maximal_segment
    fastest = 1.0 / 30.0
    forgetting_factors = jnp.exp(jax.random.uniform(jax.random.fold_in(key, 1), (ATTENTION_GROUPS, 1), jnp.float32, math.log(slowest), math.log(fastest)))
    approximate_guess = jnp.exp(jax.random.uniform(jax.random.fold_in(key, 2), (ATTENTION_GROUPS, SEQUENCE_ENTRIES), jnp.float32, -0.7, 0.7))
    segment_spans = jax.random.bernoulli(jax.random.fold_in(key, 3), 2.0 / maximal_segment, (ATTENTION_GROUPS, SEQUENCE_ENTRIES))
    objective_scores = jnp.log(jax.random.uniform(jax.random.fold_in(key, 4), (ATTENTION_GROUPS, SEQUENCE_ENTRIES), jnp.float32, 0.5, 0.8))
    return (-forgetting_factors * approximate_guess + jnp.where(segment_spans, objective_scores, 0.0)).astype(jnp.float32)


def draw_doc_start(key, part):
    key = jax.random.fold_in(key, 7)
    maximal_segment = SPAN * TOK_DEV
    lengths = jax.random.randint(jax.random.fold_in(key, 1), (SEQUENCE_ENTRIES,), TOK_DEV // 4, maximal_segment + 1)
    placed = jax.random.randint(jax.random.fold_in(key, 2), (), 0, 2)
    lengths = jnp.where(jnp.arange(SEQUENCE_ENTRIES, dtype=jnp.int32) == placed, maximal_segment, lengths).astype(jnp.int32)
    ends = jnp.cumsum(lengths).astype(jnp.int32)
    begins = jnp.concatenate([jnp.zeros((1,), jnp.int32), ends[:-1]])
    position = jnp.arange(SEQUENCE_ENTRIES, dtype=jnp.int32)
    owner = jnp.searchsorted(begins, position, side='right') - 1
    starts = begins[owner].astype(jnp.int32)
    return jnp.where(position == SEQUENCE_ENTRIES - 1, position, starts).astype(jnp.int32)


def paired_rows(key, strength):
    shape = (SEQUENCE_ENTRIES, ATTENTION_GROUPS, DH)
    queries = jnp.clip(jax.random.normal(jax.random.fold_in(key, 21), shape), -4.0, 4.0)
    key_rows = jnp.clip(jax.random.normal(jax.random.fold_in(key, 22), shape), -4.0, 4.0)
    position = jnp.arange(SEQUENCE_ENTRIES)[:, None, None]
    chosen = jnp.where(position % 29 == 5, strength, 0.0)
    signs = jnp.where(jax.random.normal(jax.random.fold_in(key, 23), shape) > 0.0, 1.0, -1.0)
    levels = 4.4 + 1.1 * jax.random.uniform(jax.random.fold_in(key, 24), (SEQUENCE_ENTRIES, ATTENTION_GROUPS, 1))
    target = signs * levels
    margin = 1.0 + 2.0 * jax.random.uniform(jax.random.fold_in(key, 25), (SEQUENCE_ENTRIES, ATTENTION_GROUPS, 1))
    shrink = 1.0 - margin / (math.sqrt(DH) * levels * levels)
    queries = queries + chosen * (target - queries)
    key_rows = key_rows + chosen * (target - key_rows)
    follow = jnp.roll(chosen, -1, axis=0)
    key_rows = key_rows + follow * (jnp.roll(target * shrink, -1, axis=0) - key_rows)
    return (queries, key_rows)


def draw_soft_query(key, part):
    strength = 0.0
    return paired_rows(key, strength)[0].astype(jnp.bfloat16)


def draw_soft_keys(key, part):
    strength = 0.0
    return paired_rows(key, strength)[1].astype(jnp.bfloat16)


def shard_levels(key, extent, cuts, low, top_value):
    level = 1.0
    for dim, shards_of in cuts:
        steps = jax.random.uniform(jax.random.fold_in(jax.random.fold_in(key, 6), dim), (shards_of,), jnp.float32, low / len(cuts), top_value / len(cuts))
        level = level * jnp.repeat(jnp.exp(steps), extent[dim] // shards_of).reshape((-1,) + (1,) * (len(extent) - 1 - dim))
    return level


def scatter_about(own_key, dims, width, limit, cuts=(), kind=jnp.bfloat16):
    result = width * jax.random.normal(own_key, dims, jnp.float32)
    if cuts:
        result = result * shard_levels(own_key, dims, cuts, -0.22, 0.18)
    return jnp.clip(result, -limit, limit).astype(kind)


def setup_inputs(seed: int = 0) -> dict:
    splits = jax.random.split(jax.random.key(seed), 12)
    lin_query = scatter_about(splits[0], (SEQUENCE_ENTRIES, ATTENTION_GROUPS, DH), 1.0, 6.0, ((0, 64), (1, 8)))
    lin_keys = scatter_about(splits[1], (SEQUENCE_ENTRIES, ATTENTION_GROUPS, DH), 0.25, 1.5, ((0, 64), (1, 8)))
    lin_values = scatter_about(splits[2], (SEQUENCE_ENTRIES, ATTENTION_GROUPS, DH), 1.0, 6.0, ((0, 64), (1, 8)))
    log_decay = draw_log_decay(jax.random.fold_in(splits[11], 71), 0)
    norm_gain = jnp.clip(1.0 + 0.18 * jax.random.normal(splits[4], (ATTENTION_GROUPS, DH), jnp.float32), 0.1, 1.9)
    lin_cotangent = scatter_about(splits[5], (SEQUENCE_ENTRIES, ATTENTION_GROUPS, DH), 1.0, 6.0, ((0, 64), (1, 8)))
    soft_query = draw_soft_query(jax.random.fold_in(splits[11], 71), 0)
    soft_keys = draw_soft_keys(jax.random.fold_in(splits[11], 71), 0)
    soft_values = scatter_about(splits[8], (SEQUENCE_ENTRIES, ATTENTION_GROUPS, DH), 1.0, 6.0, ((0, 64), (1, 8)))
    soft_cotangent = scatter_about(splits[9], (SEQUENCE_ENTRIES, ATTENTION_GROUPS, DH), 1.0, 6.0, ((0, 64), (1, 8)))
    doc_start = draw_doc_start(jax.random.fold_in(splits[11], 71), 0)
    return dict(lin_query=lin_query, lin_keys=lin_keys, lin_values=lin_values, log_decay=log_decay, norm_gain=norm_gain, lin_cotangent=lin_cotangent, soft_query=soft_query, soft_keys=soft_keys, soft_values=soft_values, soft_cotangent=soft_cotangent, doc_start=doc_start)


norm_eps = 1e-05

def rounded(value):
    return lax.optimization_barrier(value.astype(jnp.bfloat16)).astype(jnp.float32)

def local_masks(decays, starts, first_row):
    tok_rows = starts.shape[0]
    cumulative = jnp.cumsum(decays, axis=1)
    position = jnp.arange(tok_rows, dtype=jnp.int32)
    same_doc = (starts[:, None] == starts[None, :]) & (position[None, :] <= position[:, None])
    log_gap = jnp.minimum(cumulative[:, :, None] - cumulative[:, None, :], 0.0)
    within = jnp.where(same_doc[None], jnp.exp(log_gap), 0.0)
    entering = jnp.where((starts < first_row)[None, :], jnp.exp(cumulative), 0.0)
    leaving = jnp.where((starts == starts[tok_rows - 1])[None, :], jnp.exp(cumulative[:, tok_rows - 1:] - cumulative), 0.0)
    return (within, entering, leaving)

def reference(lin_query, lin_keys, lin_values, log_decay, norm_gain, lin_cotangent, soft_query, soft_keys, soft_values, soft_cotangent, doc_start):

    def to_blocks(value):
        return value.reshape((N_CTX, TOK_DEV) + value.shape[1:])
    query_blocks = to_blocks(lin_query)
    key_blocks = to_blocks(lin_keys)
    value_blocks = to_blocks(lin_values)
    decays = jnp.transpose(log_decay.reshape(ATTENTION_GROUPS, N_CTX, TOK_DEV), (1, 0, 2))
    starts = to_blocks(doc_start)
    firsts = jnp.arange(N_CTX, dtype=jnp.int32) * TOK_DEV

    def closing_of(inputs):
        decay_rows, start_rows, first_row, key_rows, value_rows = inputs
        within, entering, leaving = local_masks(decay_rows, start_rows, first_row)
        keyed = rounded(jnp.transpose(leaving)[:, :, None] * key_rows.astype(jnp.float32))
        closing = jnp.einsum('shd,she->hde', keyed, value_rows.astype(jnp.float32))
        return (entering[:, TOK_DEV - 1], closing)
    passing, closing = lax.map(closing_of, (decays, starts, firsts, key_blocks, value_blocks))

    def forward_step(state_now, inputs):
        passes, closes = inputs
        return (passes[:, None, None] * state_now + closes, state_now)
    zero_state = jnp.zeros((ATTENTION_GROUPS, DH, DH), jnp.float32)
    _, incoming = lax.scan(forward_step, zero_state, (passing, closing))

    def raw_of(inputs):
        decay_rows, start_rows, first_row, queries, key_rows, value_rows, state_in = inputs
        within, entering, leaving = local_masks(decay_rows, start_rows, first_row)
        queries = queries.astype(jnp.float32)
        scores = jnp.einsum('thd,shd->hts', queries, key_rows.astype(jnp.float32))
        attend = rounded(within * scores)
        intra = jnp.einsum('hts,she->the', attend, value_rows.astype(jnp.float32))
        inter = jnp.einsum('thd,hde->the', queries, rounded(state_in))
        return intra + jnp.transpose(entering)[:, :, None] * inter
    raw_out = lax.map(raw_of, (decays, starts, firsts, query_blocks, key_blocks, value_blocks, incoming))
    raw_out = raw_out.reshape(SEQUENCE_ENTRIES, ATTENTION_GROUPS, DH)
    gained = lin_cotangent.astype(jnp.float32) * norm_gain[None]
    squares = lax.optimization_barrier(jnp.sum(raw_out * raw_out, axis=(1, 2)))
    crossed = lax.optimization_barrier(jnp.sum(gained * raw_out, axis=(1, 2)))
    feat_count = ATTENTION_GROUPS * DH
    rscale = lax.rsqrt(squares / feat_count + norm_eps)[:, None, None]
    lin_output = (raw_out * rscale * norm_gain[None]).astype(jnp.bfloat16)
    raw_grad = (rscale * gained - raw_out * rscale ** 3 * (crossed[:, None, None] / feat_count)).astype(jnp.bfloat16)
    grad_blocks = to_blocks(raw_grad)

    def pulled_of(inputs):
        decay_rows, start_rows, first_row, queries, cotangent = inputs
        within, entering, leaving = local_masks(decay_rows, start_rows, first_row)
        carried = rounded(jnp.transpose(entering)[:, :, None] * queries.astype(jnp.float32))
        return jnp.einsum('thd,the->hde', carried, cotangent.astype(jnp.float32))
    pulled = lax.map(pulled_of, (decays, starts, firsts, query_blocks, grad_blocks))

    def backward_step(state_now, inputs):
        passes, pulls = inputs
        return (pulls + passes[:, None, None] * state_now, state_now)
    _, outgoing = lax.scan(backward_step, zero_state, (passing, pulled), reverse=True)

    def grads_of(inputs):
        decay_rows, start_rows, first_row, queries, key_rows, value_rows, cotangent, state_in, state_back = inputs
        within, entering, leaving = local_masks(decay_rows, start_rows, first_row)
        queries = queries.astype(jnp.float32)
        key_rows = key_rows.astype(jnp.float32)
        value_rows = value_rows.astype(jnp.float32)
        cotangent = cotangent.astype(jnp.float32)
        attend = rounded(within * jnp.einsum('thd,shd->hts', queries, key_rows))
        mixed = rounded(within * jnp.einsum('the,she->hts', cotangent, value_rows))
        state_low = rounded(state_in)
        back_low = rounded(state_back)
        enter_rows = jnp.transpose(entering)[:, :, None]
        leave_rows = jnp.transpose(leaving)[:, :, None]
        query_grad = jnp.einsum('hts,shd->thd', mixed, key_rows) + enter_rows * jnp.einsum('the,hde->thd', cotangent, state_low)
        key_grad = jnp.einsum('hts,thd->shd', mixed, queries) + leave_rows * jnp.einsum('she,hde->shd', value_rows, back_low)
        value_grad = jnp.einsum('hts,the->she', attend, cotangent) + leave_rows * jnp.einsum('shd,hde->she', key_rows, back_low)
        return (query_grad.astype(jnp.bfloat16), key_grad.astype(jnp.bfloat16), value_grad.astype(jnp.bfloat16))
    lin_query_grad, lin_key_grad, lin_value_grad = lax.map(grads_of, (decays, starts, firsts, query_blocks, key_blocks, value_blocks, grad_blocks, incoming, outgoing))
    span_rows = SPAN * TOK_DEV
    width_rows = span_rows + TOK_DEV
    inv_root = 1.0 / math.sqrt(DH)
    zero_rows = jnp.zeros((span_rows, ATTENTION_GROUPS, DH), jnp.bfloat16)
    keys_padded = jnp.concatenate([zero_rows, soft_keys], axis=0)
    values_padded = jnp.concatenate([zero_rows, soft_values], axis=0)
    zero_acc = jnp.zeros((span_rows + SEQUENCE_ENTRIES, ATTENTION_GROUPS, DH), jnp.float32)

    def soft_step(carry, inputs):
        key_acc, value_acc = carry
        first_row, queries, cotangent, start_rows = inputs
        key_rows = lax.dynamic_slice_in_dim(keys_padded, first_row, width_rows, 0).astype(jnp.float32)
        value_rows = lax.dynamic_slice_in_dim(values_padded, first_row, width_rows, 0).astype(jnp.float32)
        queries = queries.astype(jnp.float32)
        cotangent = cotangent.astype(jnp.float32)
        key_pos = first_row - span_rows + jnp.arange(width_rows, dtype=jnp.int32)
        query_pos = first_row + jnp.arange(TOK_DEV, dtype=jnp.int32)
        allowed = (key_pos[None, :] <= query_pos[:, None]) & (key_pos[None, :] >= start_rows[:, None])
        logits = jnp.einsum('thd,shd->hts', queries, key_rows)
        logits = jnp.where(allowed[None], logits * inv_root, -jnp.inf)
        row_top = lax.optimization_barrier(jnp.max(logits, axis=2, keepdims=True))
        expo = jnp.exp(logits - row_top)
        row_total = lax.optimization_barrier(jnp.sum(expo, axis=2, keepdims=True))
        log_total = row_top + jnp.log(row_total)
        output = (jnp.einsum('hts,she->the', rounded(expo), value_rows) / jnp.transpose(row_total, (1, 0, 2))).astype(jnp.bfloat16)
        row_delta = lax.optimization_barrier(jnp.sum(cotangent * output.astype(jnp.float32), axis=2))
        probs = jnp.exp(logits - log_total)
        cot_dots = jnp.einsum('the,she->hts', cotangent, value_rows)
        slopes = rounded(inv_root * probs * (cot_dots - jnp.transpose(row_delta)[:, :, None]))
        query_grad = jnp.einsum('hts,shd->thd', slopes, key_rows).astype(jnp.bfloat16)
        key_part = jnp.einsum('hts,thd->shd', slopes, queries)
        value_part = jnp.einsum('hts,the->she', rounded(probs), cotangent)
        key_acc = lax.dynamic_update_slice_in_dim(key_acc, lax.dynamic_slice_in_dim(key_acc, first_row, width_rows, 0) + key_part, first_row, 0)
        value_acc = lax.dynamic_update_slice_in_dim(value_acc, lax.dynamic_slice_in_dim(value_acc, first_row, width_rows, 0) + value_part, first_row, 0)
        return ((key_acc, value_acc), (output, query_grad))
    (key_acc, value_acc), (soft_output, soft_query_grad) = lax.scan(soft_step, (zero_acc, zero_acc), (firsts, to_blocks(soft_query), to_blocks(soft_cotangent), starts))
    shape_all = (SEQUENCE_ENTRIES, ATTENTION_GROUPS, DH)
    return (lin_output, lin_query_grad.reshape(shape_all), lin_key_grad.reshape(shape_all), lin_value_grad.reshape(shape_all), soft_output.reshape(shape_all), soft_query_grad.reshape(shape_all), key_acc[span_rows:].astype(jnp.bfloat16), value_acc[span_rows:].astype(jnp.bfloat16))
```

```python
import functools
import math

import jax
import jax.numpy as jnp
from jax import lax
from jax.experimental import pallas as pl
from jax.experimental.pallas import tpu as pltpu
from jax.sharding import PartitionSpec as P

SPAN = 4
NORM_EPS = 1e-05
MASKED = -1e30
MESH = pl.DeviceIdType.MESH
F32 = jnp.float32
BF16 = jnp.bfloat16

LQ, LK, LV, LC, SQ, SK, SV, SC = range(8)
O_LIN, O_LQ, O_LK, O_LV, O_SOFT, O_SQ, O_SK, O_SV = range(8)


def dot_nn(a, b):
    return lax.dot_general(a, b, (((1,), (0,)), ((), ())), preferred_element_type=F32)


def dot_nt(a, b):
    return lax.dot_general(a, b, (((1,), (1,)), ((), ())), preferred_element_type=F32)


def dot_tn(a, b):
    return lax.dot_general(a, b, (((0,), (0,)), ((), ())), preferred_element_type=F32)


def kernel(n_ctx, n_head, heads, tok, size, *refs):
    ins = refs[:8]
    ld_in, ng_in, ds_in = refs[8:11]
    outs = refs[11:19]
    (
        raw, stage, hb, kv, ldv, ngv, dsv, bias, mask, enter, leave, within,
        gacc, gsend, grecv, fsend, frecv, nsend, nrecv,
        cl, clr, ptile, comb, x0b, ssend, srecv, tsend, trecv, isend, st,
        ysend, yrecv, attend, rawo, rgrad, pu, pur, rsend, rrecv, qsend, qrecv, osend, back,
        dkp, dvp, ostage, obf,
        in_sem, out_sem, small_sem, fwd_s, fwd_r, bwd_s, bwd_r, lin_s, lin_r, y_s, y_r,
    ) = refs[19:]
    half = heads // 2
    span = SPAN * tok
    width = span + tok
    me = lax.axis_index("ctx")
    hd = lax.axis_index("head")
    k = lax.rem(me, 2)
    first = k == 0
    par = me + 1 - 2 * k
    nxt = lax.rem(me + 2, n_ctx)
    prv = lax.rem(me + n_ctx - 2, n_ctx)
    inv_root = 1.0 / math.sqrt(size)

    def rows(slot):
        return pl.ds(pl.multiple_of(slot * tok, tok), tok)

    window = pl.ds(pl.multiple_of(k * tok, tok), width)

    def remote(src, dst, send, recv, where):
        return pltpu.make_async_remote_copy(
            src_ref=src, dst_ref=dst, send_sem=send, recv_sem=recv,
            device_id=(where, hd), device_id_type=MESH,
        )

    barrier = pltpu.get_barrier_semaphore()
    for other in (par, nxt, prv):
        pl.semaphore_signal(barrier, inc=1, device_id=(other, hd), device_id_type=MESH)
    for step in range(1, n_head):
        pl.semaphore_signal(
            barrier, inc=1, device_id=(me, lax.rem(hd + step, n_head)), device_id_type=MESH
        )

    loads = {}
    for i in (SK, SV, LK, LV, LQ, SQ, SC, LC):
        loads[i] = pltpu.make_async_copy(ins[i], raw.at[i], in_sem.at[i])
    small = [
        pltpu.make_async_copy(ds_in, dsv, small_sem.at[0]),
        pltpu.make_async_copy(ld_in, ldv, small_sem.at[1]),
        pltpu.make_async_copy(ng_in, ngv, small_sem.at[2]),
    ]
    for i in (SK, SV):
        loads[i].start()
    for copy in small:
        copy.start()
    for i in (LK, LV, LQ, SQ, SC, LC):
        loads[i].start()

    def head_of(i, h):
        return stage[i, pl.ds(h, tok, stride=heads), :]

    def unpack(i):
        loads[i].wait()
        stage[i] = raw[i].astype(F32)

    for i, part in ((SK, 0), (SV, 1)):
        unpack(i)
        for h in range(heads):
            kv[h, part, rows(4 + k), :] = head_of(i, h).astype(BF16)
    pl.semaphore_wait(barrier, 2 + n_head)

    def fwd_copy(kind, h):
        if kind == 0:
            src, dst, where = 4 + k, 2 + k, nxt
        elif kind == 1:
            src, dst, where = 2 + k, k, nxt
        elif kind == 2:
            src, dst, where = 4 - k, 4 - k, par
        else:
            src, dst, where = 2 - k, 2 - k, par
        return remote(
            kv.at[h, :, rows(src), :], kv.at[h, :, rows(dst), :],
            fwd_s.at[kind, h], fwd_r.at[kind, h], where,
        )

    fwd = {(kind, h): fwd_copy(kind, h) for kind in range(4) for h in range(heads)}

    def step_a(h):
        fwd[0, h].start()

    def step_b(h):
        fwd[0, h].wait_recv()
        fwd[1, h].start()
        fwd[2, h].start()

    def step_c(h):
        fwd[1, h].wait_recv()
        fwd[3, h].start()

    def step_d(h):
        fwd[2, h].wait_recv()
        fwd[3, h].wait_recv()

    step_a(0)
    step_a(1)

    for copy in small:
        copy.wait()
    t_pos = lax.broadcasted_iota(jnp.int32, (tok, tok), 0)
    s_pos = lax.broadcasted_iota(jnp.int32, (tok, tok), 1)
    first_row = (me * tok).astype(F32)
    ds_row = jnp.broadcast_to(dsv[...].astype(F32), (tok, tok))
    ds_col = jnp.transpose(ds_row)
    mask[...] = jnp.where((ds_row == ds_col) & (s_pos <= t_pos), 1.0, 0.0)
    ds_last = jnp.broadcast_to(ds_row[:, tok - 1 :], (tok, tok))
    triangle = jnp.where(t_pos <= s_pos, 1.0, 0.0).astype(F32)
    decays = jnp.concatenate([ldv[...], jnp.zeros((8 - heads, tok), F32)], axis=0)
    cumulative = lax.dot_general(
        decays, triangle, (((1,), (0,)), ((), ())),
        precision=lax.Precision.HIGHEST, preferred_element_type=F32,
    )
    for h in range(heads):
        cum_row = jnp.broadcast_to(cumulative[h : h + 1, :], (tok, tok))
        cum_col = jnp.transpose(cum_row)
        within[h] = jnp.where(mask[...] > 0.0, jnp.exp(jnp.minimum(cum_col - cum_row, 0.0)), 0.0)
        enter[h] = jnp.where(ds_col < first_row, jnp.exp(cum_col), 0.0)
        cum_last = jnp.broadcast_to(cum_row[:, tok - 1 :], (tok, tok))
        leave[h] = jnp.where(ds_col == ds_last, jnp.exp(cum_last - cum_col), 0.0)
        ptile[0, h : h + 1, :] = enter[h, tok - 1 :, :]
    ptile[0, heads:, :] = jnp.zeros((8 - heads, size), F32)

    for i, place in ((LK, 1), (LV, 2)):
        unpack(i)
        for h in range(heads):
            hb[place, h] = head_of(i, h).astype(BF16)

    for h in range(heads):
        keyed = (leave[h] * head_of(LK, h)).astype(BF16)
        cl[h] = dot_tn(keyed, hb[2, h])
    mine = pl.ds(2 * k, half)
    theirs = pl.ds(2 * (1 - k), half)
    cl_copy = remote(cl.at[theirs], clr, lin_s.at[0], lin_r.at[0], par)
    p_copy = remote(ptile.at[0], ptile.at[1], lin_s.at[1], lin_r.at[1], par)
    cl_copy.start()
    p_copy.start()

    for i, place in ((LQ, 0), (SQ, 3), (SC, 4)):
        unpack(i)
        for h in range(heads):
            hb[place, h] = head_of(i, h).astype(BF16)
    unpack(LC)
    for h in range(heads):
        scores = dot_nt(hb[0, h], hb[1, h])
        attend[h] = (within[h] * scores).astype(BF16)
        rawo[h] = dot_nn(attend[h], hb[2, h])

    q_index = lax.broadcasted_iota(jnp.int32, (tok, width), 0) + span
    k_index = lax.broadcasted_iota(jnp.int32, (tok, width), 1)
    ds_wide = jnp.broadcast_to(ds_col[:, :1], (tok, width)) - first_row + float(span)
    allowed = (k_index <= q_index) & (k_index.astype(F32) >= ds_wide)
    bias[...] = jnp.where(allowed, 0.0, MASKED)

    def pass_rows(j):
        own = ptile[0, pl.ds(2 * k + j, 1), :]
        other = ptile[1, pl.ds(2 * k + j, 1), :]
        return jnp.where(first, own, other), jnp.where(first, other, own)

    cl_copy.wait_recv()
    p_copy.wait_recv()
    s_copy = remote(ssend, srecv, lin_s.at[2], lin_r.at[2], nxt)
    t_copy = remote(tsend, trecv, lin_s.at[3], lin_r.at[3], nxt)
    i_copy = remote(isend, st.at[mine], lin_s.at[4], lin_r.at[4], par)
    for j in range(half):
        own, other = cl[2 * k + j], clr[j]
        x0, x1 = jnp.where(first, own, other), jnp.where(first, other, own)
        p0, p1 = pass_rows(j)
        x0b[j] = x0
        comb[j] = x1 + p1 * x0
        ssend[j] = comb[j].astype(BF16)
    s_copy.start()
    step_b(0)
    step_a(2)
    s_copy.wait_recv()
    for j in range(half):
        p0, p1 = pass_rows(j)
        tsend[j] = (comb[j] + (p1 * p0) * srecv[j].astype(F32)).astype(BF16)
    t_copy.start()
    step_b(1)
    step_a(3)
    step_c(0)
    step_d(0)

    def soft(h):
        query, cot = hb[3, h], hb[4, h]
        keys, values = kv[h, 0, window, :], kv[h, 1, window, :]
        logits = dot_nt(query, keys) * inv_root + bias[...]
        top = jnp.max(logits, axis=1, keepdims=True)
        expo = jnp.exp(logits - top)
        inverse = 1.0 / jnp.sum(expo, axis=1, keepdims=True)
        out = (dot_nn(expo.astype(BF16), values) * inverse).astype(BF16).astype(F32)
        ostage[O_SOFT, pl.ds(h, tok, stride=heads), :] = out
        delta = jnp.sum(cot.astype(F32) * out, axis=1, keepdims=True)
        probs = expo * inverse
        slopes = (inv_root * probs * (dot_nt(cot, values) - delta)).astype(BF16)
        ostage[O_SQ, pl.ds(h, tok, stride=heads), :] = dot_nn(slopes, keys)
        gacc[h, 0, window, :] = dot_tn(slopes, query)
        gacc[h, 1, window, :] = dot_tn(probs.astype(BF16), cot)

    def bwd_copy(kind, h):
        if kind == 0:
            return remote(gsend.at[h], grecv.at[h], bwd_s.at[0, h], bwd_r.at[0, h], par)
        if kind == 1:
            return remote(fsend.at[h], frecv.at[h], bwd_s.at[1, h], bwd_r.at[1, h], prv)
        return remote(nsend.at[h], nrecv.at[h], bwd_s.at[2, h], bwd_r.at[2, h], prv)

    bwd = {(kind, h): bwd_copy(kind, h) for kind in range(3) for h in range(heads)}

    def step_e(h):
        for part in range(2):
            gsend[h, 0, part] = gacc[h, part, rows(1 + k), :].astype(BF16)
            gsend[h, 1, part] = gacc[h, part, rows(3 + k), :].astype(BF16)
        bwd[0, h].start()

    def step_f(h):
        bwd[0, h].wait_recv()
        for part in range(2):
            gacc[h, part, rows(2 - k), :] += grecv[h, 0, part].astype(F32)
            gacc[h, part, rows(4 - k), :] += grecv[h, 1, part].astype(F32)
            fsend[h, part] = gacc[h, part, rows(k), :].astype(BF16)
        bwd[1, h].start()

    def step_g(h):
        bwd[1, h].wait_recv()
        for part in range(2):
            nsend[h, part] = (
                gacc[h, part, rows(2 + k), :] + frecv[h, part].astype(F32)
            ).astype(BF16)
        bwd[2, h].start()

    def step_h(h):
        bwd[2, h].wait_recv()
        for part, place in ((0, O_SK), (1, O_SV)):
            ostage[place, pl.ds(h, tok, stride=heads), :] = (
                gacc[h, part, rows(4 + k), :] + nrecv[h, part].astype(F32)
            )

    out_copies = []

    def store(i):
        obf[i] = ostage[i].astype(BF16)
        copy = pltpu.make_async_copy(obf.at[i], outs[i], out_sem.at[i])
        copy.start()
        out_copies.append(copy)

    soft(0)
    step_e(0)
    step_b(2)
    step_c(1)

    t_copy.wait_recv()
    for j in range(half):
        p0, p1 = pass_rows(j)
        in0 = trecv[j].astype(F32)
        in1 = x0b[j] + p0 * in0
        st[2 * k + j] = jnp.where(first, in0, in1).astype(BF16)
        isend[j] = jnp.where(first, in1, in0).astype(BF16)
    i_copy.start()
    step_d(1)
    step_f(0)
    soft(1)
    step_e(1)
    step_b(3)
    step_c(2)

    i_copy.wait_recv()
    squares = jnp.zeros((tok, size), F32)
    crossed = jnp.zeros((tok, size), F32)
    for h in range(heads):
        value = rawo[h] + enter[h] * dot_nn(hb[0, h], st[h])
        rawo[h] = value
        squares += value * value
        crossed += head_of(LC, h) * ngv[h : h + 1, :] * value
    ysend[0:1, :] = jnp.sum(jnp.transpose(squares), axis=0, keepdims=True)
    ysend[1:2, :] = jnp.sum(jnp.transpose(crossed), axis=0, keepdims=True)
    ysend[2:, :] = jnp.zeros((6, tok), F32)
    y_copies = []
    for step in range(1, n_head):
        y_copies.append(
            pltpu.make_async_remote_copy(
                src_ref=ysend, dst_ref=yrecv.at[step], send_sem=y_s.at[step], recv_sem=y_r.at[step],
                device_id=(me, lax.rem(hd + step, n_head)), device_id_type=MESH,
            )
        )
        y_copies[-1].start()
    step_f(1)
    step_g(0)
    step_d(2)
    soft(2)
    step_e(2)
    step_c(3)

    total = ysend[...]
    for step in range(1, n_head):
        y_copies[step - 1].wait_recv()
        total += yrecv[step]
    count = heads * size * n_head
    rscale_row = lax.rsqrt(total[0:1, :] / count + NORM_EPS)
    factor_row = rscale_row * rscale_row * rscale_row * (total[1:2, :] / count)
    rscale = jnp.transpose(jnp.broadcast_to(rscale_row, (tok, tok)))
    factor = jnp.transpose(jnp.broadcast_to(factor_row, (tok, tok)))
    for h in range(heads):
        gain = ngv[h : h + 1, :]
        value = rawo[h]
        ostage[O_LIN, pl.ds(h, tok, stride=heads), :] = value * rscale * gain
        grad = (rscale * (head_of(LC, h) * gain) - value * factor).astype(BF16)
        rgrad[h] = grad
        carried = (enter[h] * hb[0, h].astype(F32)).astype(BF16)
        pu[h] = dot_tn(carried, grad)
    pu_copy = remote(pu.at[theirs], pur, lin_s.at[5], lin_r.at[5], par)
    pu_copy.start()
    store(O_LIN)
    step_f(2)
    step_g(1)
    step_h(0)
    step_d(3)

    pu_copy.wait_recv()
    r_copy = remote(rsend, rrecv, lin_s.at[6], lin_r.at[6], prv)
    q_copy = remote(qsend, qrecv, lin_s.at[7], lin_r.at[7], prv)
    o_copy = remote(osend, back.at[mine], lin_s.at[8], lin_r.at[8], par)
    for j in range(half):
        own, other = pu[2 * k + j], pur[j]
        y0, y1 = jnp.where(first, own, other), jnp.where(first, other, own)
        p0, p1 = pass_rows(j)
        x0b[j] = y1
        comb[j] = y0 + p0 * y1
        rsend[j] = comb[j].astype(BF16)
    r_copy.start()

    soft(3)
    step_e(3)

    r_copy.wait_recv()
    for j in range(half):
        p0, p1 = pass_rows(j)
        qsend[j] = (comb[j] + (p0 * p1) * rrecv[j].astype(F32)).astype(BF16)
    q_copy.start()
    step_f(3)
    step_g(2)
    step_h(1)
    store(O_SOFT)
    store(O_SQ)

    for h in range(heads):
        query, key, value, grad = hb[0, h], hb[1, h], hb[2, h], rgrad[h]
        mixed = (within[h] * dot_nt(grad, value)).astype(BF16)
        ostage[O_LQ, pl.ds(h, tok, stride=heads), :] = dot_nn(mixed, key) + enter[h] * dot_nt(
            grad, st[h]
        )
        dkp[h] = dot_tn(mixed, query)
        dvp[h] = dot_tn(attend[h], grad)
    store(O_LQ)

    q_copy.wait_recv()
    for j in range(half):
        p0, p1 = pass_rows(j)
        out1 = qrecv[j].astype(F32)
        out0 = x0b[j] + p1 * out1
        back[2 * k + j] = jnp.where(first, out0, out1).astype(BF16)
        osend[j] = jnp.where(first, out1, out0).astype(BF16)
    o_copy.start()
    step_g(3)
    step_h(2)

    o_copy.wait_recv()
    for h in range(heads):
        ostage[O_LK, pl.ds(h, tok, stride=heads), :] = dkp[h] + leave[h] * dot_nt(
            hb[2, h], back[h]
        )
        ostage[O_LV, pl.ds(h, tok, stride=heads), :] = dvp[h] + leave[h] * dot_nn(
            hb[1, h], back[h]
        )
    store(O_LK)
    store(O_LV)
    step_h(3)
    store(O_SK)
    store(O_SV)

    for copy in list(fwd.values()) + list(bwd.values()) + y_copies:
        copy.wait_send()
    for copy in (cl_copy, p_copy, s_copy, t_copy, i_copy, pu_copy, r_copy, q_copy, o_copy):
        copy.wait_send()
    for copy in out_copies:
        copy.wait()


def write_out(*refs):
    copies = [pltpu.make_async_copy(refs[i], refs[8 + i], refs[16].at[i]) for i in range(8)]
    for copy in copies:
        copy.start()
    for copy in copies:
        copy.wait()


def shards(n_ctx, n_head, *args):
    tok, heads, size = args[0].shape
    (lq, lk, lv, ld, ng, lc, sq, sk, sv, sc, ds) = args
    flat = (tok * heads, size)
    big = [a.reshape(flat) for a in (lq, lk, lv, lc, sq, sk, sv, sc)]
    square = (heads, tok, size)
    half = (heads // 2, size, size)
    wide = (heads, 2, (SPAN + 2) * tok, size)
    vmem = pltpu.VMEM
    dma = pltpu.SemaphoreType.DMA
    any_spec = pl.BlockSpec(memory_space=pl.ANY)
    pair = (heads, 2, tok, size)
    scratch = [
        vmem((8,) + flat, BF16),
        vmem((8,) + flat, F32),
        vmem((5,) + square, BF16),
        vmem(wide, BF16),
        vmem((heads, tok), F32),
        vmem((heads, size), F32),
        vmem((1, tok), jnp.int32),
        vmem((tok, (SPAN + 1) * tok), F32),
        vmem((tok, tok), F32),
        vmem(square, F32),
        vmem(square, F32),
        vmem(square, F32),
        vmem(wide, F32),
        vmem((heads, 2, 2, tok, size), BF16),
        vmem((heads, 2, 2, tok, size), BF16),
        vmem(pair, BF16),
        vmem(pair, BF16),
        vmem(pair, BF16),
        vmem(pair, BF16),
        vmem((heads, size, size), F32),
        vmem(half, F32),
        vmem((2, 8, size), F32),
        vmem(half, F32),
        vmem(half, F32),
        vmem(half, BF16),
        vmem(half, BF16),
        vmem(half, BF16),
        vmem(half, BF16),
        vmem(half, BF16),
        vmem((heads, size, size), BF16),
        vmem((8, tok), F32),
        vmem((n_head, 8, tok), F32),
        vmem((heads, tok, tok), BF16),
        vmem(square, F32),
        vmem(square, BF16),
        vmem((heads, size, size), F32),
        vmem(half, F32),
        vmem(half, BF16),
        vmem(half, BF16),
        vmem(half, BF16),
        vmem(half, BF16),
        vmem(half, BF16),
        vmem((heads, size, size), BF16),
        vmem(square, F32),
        vmem(square, F32),
        vmem((8,) + flat, F32),
        vmem((8,) + flat, BF16),
        dma((8,)),
        dma((8,)),
        dma((3,)),
        dma((4, heads)),
        dma((4, heads)),
        dma((3, heads)),
        dma((3, heads)),
        dma((9,)),
        dma((9,)),
        dma((n_head,)),
        dma((n_head,)),
    ]
    results = pl.pallas_call(
        functools.partial(kernel, n_ctx, n_head, heads, tok, size),
        out_shape=[vmem(flat, BF16)] * 8,
        in_specs=[any_spec] * 11,
        out_specs=[any_spec] * 8,
        scratch_shapes=scratch,
        compiler_params=pltpu.CompilerParams(
            collective_id=0, has_side_effects=True, vmem_limit_bytes=48 * 1024 * 1024
        ),
    )(*[pltpu.with_memory_space_constraint(a, pltpu.HBM) for a in (*big, ld, ng, ds.reshape(1, tok))])
    results = pl.pallas_call(
        write_out,
        out_shape=[jax.ShapeDtypeStruct(flat, BF16)] * 8,
        in_specs=[any_spec] * 8,
        out_specs=[any_spec] * 8,
        scratch_shapes=[dma((8,))],
    )(*[pltpu.with_memory_space_constraint(r, pltpu.VMEM) for r in results])
    return tuple(r.reshape(tok, heads, size) for r in results)


def solution(mesh):
    cube = P("ctx", "head", None)
    in_specs = (
        cube, cube, cube, P("head", "ctx"), P("head", None), cube, cube, cube, cube, cube, P("ctx"),
    )
    return jax.shard_map(
        functools.partial(shards, mesh.shape["ctx"], mesh.shape["head"]),
        mesh=mesh, in_specs=in_specs, out_specs=(cube,) * 8, check_vma=False,
    )
```

```python
import functools
import math

import jax
import jax.numpy as jnp
from jax import lax
from jax.experimental import pallas as pl
from jax.experimental.pallas import tpu as pltpu
from jax.sharding import PartitionSpec as P

SPAN = 4
NORM_EPS = 1e-05
MASKED = -1e30
MESH = pl.DeviceIdType.MESH
F32 = jnp.float32
BF16 = jnp.bfloat16

LQ, LK, LV, LC, SQ, SK, SV, SC = range(8)
O_LIN, O_LQ, O_LK, O_LV, O_SOFT, O_SQ, O_SK, O_SV = range(8)


DIRECT_KV = ()


def dot_nn(a, b):
    return lax.dot_general(a, b, (((1,), (0,)), ((), ())), preferred_element_type=F32)


def dot_nt(a, b):
    return lax.dot_general(a, b, (((1,), (1,)), ((), ())), preferred_element_type=F32)


def dot_tn(a, b):
    return lax.dot_general(a, b, (((0,), (0,)), ((), ())), preferred_element_type=F32)


def kernel(n_ctx, n_head, heads, tok, size, *refs):
    ins = refs[:8]
    ld_in, ng_in, ds_in = refs[8:11]
    outs = refs[11:19]
    (
        raw, stage, hb, kv, ldv, ngv, dsv, bias, bias_t, mask, enter, leave, within,
        qd, stats,
        cl, clr, ptile, pprod, x0b, comb, ssend, snear, tsend, sfar, isend, st,
        ysend, yrecv, attend, rawo, rgrad, pu, pur, rsend, rnear, rfar, osend, back,
        dkp, dvp, ostage,
        in_sem, small_sem, fwd_s, fwd_r, bwd_s, bwd_r, st_s, st_r, lin_s, lin_r, y_s, y_r,
    ) = refs[19:]
    half = heads // 2
    span = SPAN * tok
    width = span + tok
    me = lax.axis_index("ctx")
    hd = lax.axis_index("head")
    k = lax.rem(me, 2)
    first = k == 0
    par = me + 1 - 2 * k
    nxt = lax.rem(me + 2, n_ctx)
    prv = lax.rem(me + n_ctx - 2, n_ctx)
    nxt2 = lax.rem(me + 4, n_ctx)
    prv2 = lax.rem(me + n_ctx - 4, n_ctx)
    inv_root = 1.0 / math.sqrt(size)

    def window(ref, h, part):
        return ref[h, pl.ds(k, SPAN + 1), part].reshape(width, size)

    mine = pl.ds(2 * k, half)
    theirs = pl.ds(2 * (1 - k), half)

    copies = {}

    def remote(name, src, dst, send, recv, where):
        copies[name] = pltpu.make_async_remote_copy(
            src_ref=src, dst_ref=dst, send_sem=send, recv_sem=recv,
            device_id=where, device_id_type=MESH,
        )

    barrier = pltpu.get_barrier_semaphore()
    before = [lax.rem(me + n_ctx - step, n_ctx) for step in range(1, SPAN + 1)]
    after = [lax.rem(me + step, n_ctx) for step in range(1, SPAN + 1)]
    for other in before + after:
        pl.semaphore_signal(barrier, inc=1, device_id=(other, hd), device_id_type=MESH)
    peers = [(me, lax.rem(hd + step, n_head)) for step in range(1, n_head)]
    for peer in peers:
        pl.semaphore_signal(barrier, inc=1, device_id=peer, device_id_type=MESH)

    loads = [pltpu.make_async_copy(ins[i], raw.at[i], in_sem.at[i]) for i in range(8)]
    small = [
        pltpu.make_async_copy(ds_in, dsv, small_sem.at[0]),
        pltpu.make_async_copy(ld_in, ldv, small_sem.at[1]),
        pltpu.make_async_copy(ng_in, ngv, small_sem.at[2]),
    ]
    for copy in small:
        copy.start()
    for i in (LK, LV, SK, SV):
        loads[i].start()
    for i in (SQ, SC, LQ, LC):
        loads[i].start()

    for h in range(heads):
        whole = kv.at[h]

        def block(slot):
            return whole.at[slot]

        sems = [(fwd_s.at[kind, h], fwd_r.at[kind, h]) for kind in range(4)]
        remote(("near", h), block(4 + k), block(2 + k), *sems[0], (nxt, hd))
        if h in DIRECT_KV:
            remote(("far", h), block(4 + k), block(k), *sems[1], (nxt2, hd))
        else:
            remote(("far", h), block(2 + k), block(k), *sems[1], (nxt, hd))
        remote(("core", h), block(4 - k), block(4 - k), *sems[2], (par, hd))
        remote(("core2", h), block(2 - k), block(2 - k), *sems[3], (par, hd))
        queries = qd.at[h]

        def qblock(slot):
            return queries.at[slot]

        sems = [(bwd_s.at[kind, h], bwd_r.at[kind, h]) for kind in range(4)]
        remote(("qnear", h), qblock(k), qblock(2 + k), *sems[0], (prv, hd))
        remote(("qfar", h), qblock(2 + k), qblock(4 + k), *sems[1], (prv, hd))
        remote(("qcore", h), qblock(2 - k), qblock(2 - k), *sems[2], (par, hd))
        remote(("qcore2", h), qblock(4 - k), qblock(4 - k), *sems[3], (par, hd))
        for i in range(SPAN):
            remote(
                ("stats", h, i), stats.at[h, 0], stats.at[h, i + 1],
                st_s.at[i, h], st_r.at[i, h], (before[i], hd),
            )
    lin = [
        ("closing", cl.at[theirs], clr, par),
        ("pass", ptile.at[0], ptile.at[1], par),
        ("pprev", pprod.at[0], pprod.at[1], prv),
        ("snear", ssend, snear, nxt),
        ("sfar", tsend, sfar, nxt),
        ("state", isend, st.at[mine], par),
        ("pulled", pu.at[theirs], pur, par),
        ("rnear", rsend, rnear, prv),
        ("rfar", rsend, rfar, prv2),
        ("back", osend, back.at[mine], par),
    ]
    for i, (name, src, dst, where) in enumerate(lin):
        remote(name, src, dst, lin_s.at[i], lin_r.at[i], (where, hd))
    for step, peer in enumerate(peers):
        remote(("sums", step), ysend, yrecv.at[step], y_s.at[step], y_r.at[step], peer)

    def head_of(i, h):
        return stage[i, pl.ds(h, tok, stride=heads), :]

    def unpack(i, place):
        loads[i].wait()
        stage[i] = raw[i].astype(F32)
        for h in range(heads):
            if place is not None:
                hb[place, h] = head_of(i, h).astype(BF16)

    def put(place, h, value):
        ostage[place, pl.ds(h, tok, stride=heads), :] = value

    def finish(place):
        outs[place][...] = ostage[place].astype(BF16)

    def pass_rows(j):
        own = ptile[0, pl.ds(2 * k + j, 1), :]
        other = ptile[1, pl.ds(2 * k + j, 1), :]
        return jnp.where(first, own, other), jnp.where(first, other, own)

    def load_kv():
        for i, part in ((SK, 0), (SV, 1)):
            loads[i].wait()
            stage[i] = raw[i].astype(F32)
            for h in range(heads):
                kv[h, 4 + k, part] = head_of(i, h).astype(BF16)

    def load_qd():
        for i, part in ((SQ, 0), (SC, 1)):
            loads[i].wait()
            stage[i] = raw[i].astype(F32)
            for h in range(heads):
                qd[h, k, part] = head_of(i, h).astype(BF16)

    def send_qd(h):
        copies["qnear", h].start()

    def qrelay(h):
        copies["qnear", h].wait_recv()
        copies["qfar", h].start()
        copies["qcore", h].start()

    def qrelay_core(h):
        copies["qfar", h].wait_recv()
        copies["qcore2", h].start()

    def enter_kernel():
        pl.semaphore_wait(barrier, 2 * SPAN + n_head - 1)

    def send_own(h):
        copies["near", h].start()
        if h in DIRECT_KV:
            copies["far", h].start()

    def relay(h):
        copies["near", h].wait_recv()
        if h not in DIRECT_KV:
            copies["far", h].start()
        copies["core", h].start()

    def relay_core(h):
        copies["far", h].wait_recv()
        copies["core2", h].start()

    def soft(h):
        copies["core", h].wait_recv()
        copies["core2", h].wait_recv()
        query, cot = qd[h, k, 0], qd[h, k, 1]
        keys, values = window(kv, h, 0), window(kv, h, 1)
        logits = dot_nt(query, keys) * inv_root + bias[...]
        top = jnp.max(logits, axis=1, keepdims=True)
        expo = jnp.exp(logits - top)
        total = jnp.sum(expo, axis=1, keepdims=True)
        inverse = 1.0 / total
        out = (dot_nn(expo.astype(BF16), values) * inverse).astype(BF16).astype(F32)
        put(O_SOFT, h, out)
        delta = jnp.sum(cot.astype(F32) * out, axis=1, keepdims=True)
        lane = lax.broadcasted_iota(jnp.int32, (tok, tok), 1)
        figures = jnp.where(lane == 0, top + jnp.log(total), jnp.where(lane == 1, delta, mask[1]))
        stats[h, 0] = jnp.transpose(figures)[:8, :]
        for i in range(SPAN):
            copies["stats", h, i].start()
        slopes = inv_root * (expo * inverse) * (dot_nt(cot, values) - delta)
        put(O_SQ, h, dot_nn(slopes.astype(BF16), keys))

    def soft_grad(h):
        copies["qcore", h].wait_recv()
        copies["qcore2", h].wait_recv()
        if h > 0:
            for i in range(SPAN):
                copies["stats", h, i].wait_recv()
        keys, values = kv[h, 4 + k, 0], kv[h, 4 + k, 1]
        queries, cots = window(qd, h, 0), window(qd, h, 1)
        wide = [
            jnp.concatenate([stats[h, i, row : row + 1, :] for i in range(SPAN + 1)], axis=1)
            for row in range(2)
        ]
        logits = dot_nt(keys, queries) * inv_root + bias_t[...]
        probs = jnp.exp(logits - wide[0])
        put(O_SV, h, dot_nn(probs.astype(BF16), cots))
        slopes = inv_root * probs * (dot_nt(values, cots) - wide[1])
        put(O_SK, h, dot_nn(slopes.astype(BF16), queries))

    def later_mask():
        for i in range(SPAN):
            copies["stats", 0, i].wait_recv()
        k_index = lax.broadcasted_iota(jnp.int32, (tok, width), 0)
        q_index = lax.broadcasted_iota(jnp.int32, (tok, width), 1)
        starts = jnp.concatenate([stats[0, i, 2:3, :] for i in range(SPAN + 1)], axis=1)
        position = k_index.astype(F32) + (me * tok).astype(F32)
        inside = q_index < (n_ctx - me) * tok
        allowed = (k_index <= q_index) & (position >= starts) & inside
        bias_t[...] = jnp.where(allowed, 0.0, MASKED)

    def decays():
        for copy in small:
            copy.wait()
        t_pos = lax.broadcasted_iota(jnp.int32, (tok, tok), 0)
        s_pos = lax.broadcasted_iota(jnp.int32, (tok, tok), 1)
        first_row = (me * tok).astype(F32)
        ds_row = jnp.broadcast_to(dsv[...].astype(F32), (tok, tok))
        ds_col = jnp.transpose(ds_row)
        mask[0] = jnp.where((ds_row == ds_col) & (s_pos <= t_pos), 1.0, 0.0)
        mask[1] = ds_col
        ds_last = jnp.broadcast_to(ds_row[:, tok - 1 :], (tok, tok))
        triangle = jnp.where(t_pos <= s_pos, 1.0, 0.0).astype(F32)
        logs = jnp.concatenate([ldv[...], jnp.zeros((8 - heads, tok), F32)], axis=0)
        cumulative = lax.dot_general(
            logs, triangle, (((1,), (0,)), ((), ())),
            precision=lax.Precision.HIGHEST, preferred_element_type=F32,
        )
        for h in range(heads):
            cum_row = jnp.broadcast_to(cumulative[h : h + 1, :], (tok, tok))
            cum_col = jnp.transpose(cum_row)
            gap = jnp.exp(jnp.minimum(cum_col - cum_row, 0.0))
            within[h] = jnp.where(mask[0] > 0.0, gap, 0.0)
            enter[h] = jnp.where(ds_col < first_row, jnp.exp(cum_col), 0.0)
            cum_last = jnp.broadcast_to(cum_row[:, tok - 1 :], (tok, tok))
            leave[h] = jnp.where(ds_col == ds_last, jnp.exp(cum_last - cum_col), 0.0)
            ptile[0, h : h + 1, :] = enter[h, tok - 1 :, :]
        ptile[0, heads:, :] = jnp.zeros((8 - heads, size), F32)

    def closing():
        unpack(LK, 1)
        unpack(LV, 2)
        for h in range(heads):
            keyed = (leave[h] * head_of(LK, h)).astype(BF16)
            cl[h] = dot_tn(keyed, hb[2, h])

    def send_closing():
        copies["closing"].start()
        copies["pass"].start()

    def local_lin():
        unpack(LQ, 0)
        for h in range(heads):
            attend[h] = (within[h] * dot_nt(hb[0, h], hb[1, h])).astype(BF16)
            rawo[h] = dot_nn(attend[h], hb[2, h])
        unpack(LC, None)

    def local_soft():
        q_index = lax.broadcasted_iota(jnp.int32, (tok, width), 0) + span
        k_index = lax.broadcasted_iota(jnp.int32, (tok, width), 1)
        starts = jnp.concatenate([mask[1]] * (width // tok), axis=1)
        position = k_index.astype(F32) + (me * tok - span).astype(F32)
        allowed = (k_index <= q_index) & (position >= starts)
        bias[...] = jnp.where(allowed, 0.0, MASKED)

    def state_send():
        copies["pass"].wait_recv()
        pprod[0] = ptile[0] * ptile[1]
        copies["closing"].wait_recv()
        for j in range(half):
            own, other = cl[2 * k + j], clr[j]
            x0, x1 = jnp.where(first, own, other), jnp.where(first, other, own)
            p0, p1 = pass_rows(j)
            x0b[j] = x0
            comb[j] = x1 + p1 * x0
            ssend[j] = comb[j].astype(BF16)
        copies["snear"].start()
        copies["pprev"].start()

    def state_relay():
        copies["snear"].wait_recv()
        for j in range(half):
            both = pprod[0, pl.ds(2 * k + j, 1), :]
            tsend[j] = (comb[j] + both * snear[j].astype(F32)).astype(BF16)
        copies["sfar"].start()

    def state_get():
        copies["sfar"].wait_recv()
        for j in range(half):
            p0, p1 = pass_rows(j)
            in0 = sfar[j].astype(F32)
            in1 = x0b[j] + p0 * in0
            st[2 * k + j] = jnp.where(first, in0, in1).astype(BF16)
            isend[j] = jnp.where(first, in1, in0).astype(BF16)
        copies["state"].start()

    def lin_raw():
        copies["state"].wait_recv()
        squares = jnp.zeros((tok, size), F32)
        crossed = jnp.zeros((tok, size), F32)
        for h in range(heads):
            value = rawo[h] + enter[h] * dot_nn(hb[0, h], st[h])
            rawo[h] = value
            squares += value * value
            crossed += head_of(LC, h) * ngv[h : h + 1, :] * value
        ysend[0:1, :] = jnp.sum(jnp.transpose(squares), axis=0, keepdims=True)
        ysend[1:2, :] = jnp.sum(jnp.transpose(crossed), axis=0, keepdims=True)
        ysend[2:, :] = jnp.zeros((6, tok), F32)
        for step in range(n_head - 1):
            copies["sums", step].start()

    def lin_norm():
        total = ysend[...]
        for step in range(n_head - 1):
            copies["sums", step].wait_recv()
            total += yrecv[step]
        count = heads * size * n_head
        rscale_row = lax.rsqrt(total[0:1, :] / count + NORM_EPS)
        factor_row = rscale_row * rscale_row * rscale_row * (total[1:2, :] / count)
        rscale = jnp.transpose(jnp.broadcast_to(rscale_row, (tok, tok)))
        factor = jnp.transpose(jnp.broadcast_to(factor_row, (tok, tok)))
        for h in range(heads):
            gain = ngv[h : h + 1, :]
            value = rawo[h]
            put(O_LIN, h, value * rscale * gain)
            grad = (rscale * (head_of(LC, h) * gain) - value * factor).astype(BF16)
            rgrad[h] = grad
            carried = (enter[h] * hb[0, h].astype(F32)).astype(BF16)
            pu[h] = dot_tn(carried, grad)
        copies["pulled"].start()

    def back_send():
        copies["pulled"].wait_recv()
        for j in range(half):
            own, other = pu[2 * k + j], pur[j]
            y0, y1 = jnp.where(first, own, other), jnp.where(first, other, own)
            p0, p1 = pass_rows(j)
            x0b[j] = y1
            rsend[j] = (y0 + p0 * y1).astype(BF16)
        copies["rnear"].start()
        copies["rfar"].start()

    def back_get():
        for name in ("rnear", "rfar", "pprev"):
            copies[name].wait_recv()
        for j in range(half):
            p0, p1 = pass_rows(j)
            out1 = rnear[j].astype(F32) + pprod[1, pl.ds(2 * k + j, 1), :] * rfar[j].astype(F32)
            out0 = x0b[j] + p1 * out1
            back[2 * k + j] = jnp.where(first, out0, out1).astype(BF16)
            osend[j] = jnp.where(first, out1, out0).astype(BF16)
        copies["back"].start()

    def lin_local_grads():
        for h in range(heads):
            query, key, value, grad = hb[0, h], hb[1, h], hb[2, h], rgrad[h]
            mixed = (within[h] * dot_nt(grad, value)).astype(BF16)
            put(O_LQ, h, dot_nn(mixed, key) + enter[h] * dot_nt(grad, st[h]))
            dkp[h] = dot_tn(mixed, query)
            dvp[h] = dot_tn(attend[h], grad)

    def lin_grads():
        copies["back"].wait_recv()
        for h in range(heads):
            put(O_LK, h, dkp[h] + leave[h] * dot_nt(hb[2, h], back[h]))
            put(O_LV, h, dvp[h] + leave[h] * dot_nn(hb[1, h], back[h]))

    decays()
    closing()
    enter_kernel()
    send_closing()
    load_kv()
    send_own(0)
    load_qd()
    send_qd(0)
    send_qd(1)
    local_lin()
    state_send()
    send_own(1)
    send_qd(2)
    local_soft()
    relay(0)
    send_own(2)
    state_relay()
    send_qd(3)
    relay(1)
    send_own(3)
    qrelay(0)
    qrelay(1)
    qrelay(2)
    state_get()
    relay(2)
    qrelay(3)
    relay_core(0)
    lin_raw()
    relay(3)
    relay_core(1)
    soft(0)
    qrelay_core(0)
    qrelay_core(1)
    relay_core(2)
    soft(1)
    qrelay_core(2)
    lin_norm()
    relay_core(3)
    soft(2)
    back_send()
    qrelay_core(3)
    soft(3)
    later_mask()
    soft_grad(0)
    finish(0)
    finish(4)
    finish(5)
    lin_local_grads()
    finish(1)
    soft_grad(1)
    soft_grad(2)
    back_get()
    soft_grad(3)
    finish(6)
    finish(7)
    lin_grads()
    finish(2)
    finish(3)
    for copy in copies.values():
        copy.wait_send()


def write_out(*refs):
    copies = [pltpu.make_async_copy(refs[i], refs[8 + i], refs[16].at[i]) for i in range(8)]
    for copy in copies:
        copy.start()
    for copy in copies:
        copy.wait()


def shards(n_ctx, n_head, *args):
    tok, heads, size = args[0].shape
    (lq, lk, lv, ld, ng, lc, sq, sk, sv, sc, ds) = args
    flat = (tok * heads, size)
    big = [a.reshape(flat) for a in (lq, lk, lv, lc, sq, sk, sv, sc)]
    square = (heads, tok, size)
    half = (heads // 2, size, size)
    wide = (heads, SPAN + 2, 2, tok, size)
    vmem = pltpu.VMEM
    dma = pltpu.SemaphoreType.DMA
    any_spec = pl.BlockSpec(memory_space=pl.ANY)
    pair = (heads, 2, tok, size)
    scratch = [
        vmem((8,) + flat, BF16),
        vmem((8,) + flat, F32),
        vmem((3,) + square, BF16),
        vmem(wide, BF16),
        vmem((heads, tok), F32),
        vmem((heads, size), F32),
        vmem((1, tok), jnp.int32),
        vmem((tok, (SPAN + 1) * tok), F32),
        vmem((tok, (SPAN + 1) * tok), F32),
        vmem((2, tok, tok), F32),
        vmem(square, F32),
        vmem(square, F32),
        vmem(square, F32),
        vmem(wide, BF16),
        vmem((heads, SPAN + 1, 8, tok), F32),
        vmem((heads, size, size), F32),
        vmem(half, F32),
        vmem((2, 8, size), F32),
        vmem((2, 8, size), F32),
        vmem(half, F32),
        vmem(half, F32),
        vmem(half, BF16),
        vmem(half, BF16),
        vmem(half, BF16),
        vmem(half, BF16),
        vmem(half, BF16),
        vmem((heads, size, size), BF16),
        vmem((8, tok), F32),
        vmem((n_head, 8, tok), F32),
        vmem((heads, tok, tok), BF16),
        vmem(square, F32),
        vmem(square, BF16),
        vmem((heads, size, size), F32),
        vmem(half, F32),
        vmem(half, BF16),
        vmem(half, BF16),
        vmem(half, BF16),
        vmem(half, BF16),
        vmem((heads, size, size), BF16),
        vmem(square, F32),
        vmem(square, F32),
        vmem((8,) + flat, F32),
        dma((8,)),
        dma((3,)),
        dma((4, heads)),
        dma((4, heads)),
        dma((4, heads)),
        dma((4, heads)),
        dma((SPAN, heads)),
        dma((SPAN, heads)),
        dma((10,)),
        dma((10,)),
        dma((n_head,)),
        dma((n_head,)),
    ]
    results = pl.pallas_call(
        functools.partial(kernel, n_ctx, n_head, heads, tok, size),
        out_shape=[vmem(flat, BF16)] * 8,
        in_specs=[any_spec] * 11,
        out_specs=[pl.BlockSpec(memory_space=pltpu.VMEM)] * 8,
        scratch_shapes=scratch,
        compiler_params=pltpu.CompilerParams(
            collective_id=0, has_side_effects=True, vmem_limit_bytes=48 * 1024 * 1024
        ),
    )(*[pltpu.with_memory_space_constraint(a, pltpu.HBM) for a in (*big, ld, ng, ds.reshape(1, tok))])
    results = pl.pallas_call(
        write_out,
        out_shape=[jax.ShapeDtypeStruct(flat, BF16)] * 8,
        in_specs=[any_spec] * 8,
        out_specs=[any_spec] * 8,
        scratch_shapes=[dma((8,))],
    )(*[pltpu.with_memory_space_constraint(r, pltpu.VMEM) for r in results])
    return tuple(r.reshape(tok, heads, size) for r in results)


def solution(mesh):
    cube = P("ctx", "head", None)
    in_specs = (
        cube, cube, cube, P("head", "ctx"), P("head", None), cube, cube, cube, cube, cube, P("ctx"),
    )
    return jax.shard_map(
        functools.partial(shards, mesh.shape["ctx"], mesh.shape["head"]),
        mesh=mesh, in_specs=in_specs, out_specs=(cube,) * 8, check_vma=False,
    )
```

```python
import functools
import math

import jax
import jax.numpy as jnp
from jax import lax
from jax.experimental import pallas as pl
from jax.experimental.pallas import tpu as pltpu
from jax.sharding import PartitionSpec as P

SPAN = 4
NORM_EPS = 1e-05
MASKED = -1e30
MESH = pl.DeviceIdType.MESH
F32 = jnp.float32
BF16 = jnp.bfloat16

LQ, LK, LV, LC, SQ, SK, SV, SC = range(8)
O_LIN, O_LQ, O_LK, O_LV, O_SOFT, O_SQ, O_SK, O_SV = range(8)


def dot_nn(a, b):
    return lax.dot_general(a, b, (((1,), (0,)), ((), ())), preferred_element_type=F32)


def dot_nt(a, b):
    return lax.dot_general(a, b, (((1,), (1,)), ((), ())), preferred_element_type=F32)


def dot_tn(a, b):
    return lax.dot_general(a, b, (((0,), (0,)), ((), ())), preferred_element_type=F32)


def kernel(n_ctx, n_head, heads, tok, size, *refs):
    ins = refs[:8]
    ld_in, ng_in, ds_in = refs[8:11]
    outs = refs[11:19]
    (
        raw, stage, hb, kv, ldv, ngv, dsv, bias, bias_t, mask, enter, leave, within,
        qd, stats,
        cl, clr, ptile, pprod, x0b, comb, ssend, snear, tsend, sfar, isend, st,
        ysend, yrecv, attend, rawo, rgrad, pu, pur, rsend, rnear, qsend, rfar, osend, back,
        dkp, dvp, ostage,
        in_sem, small_sem, v_r, fwd_s, fwd_r, bwd_s, bwd_r, st_s, st_r, lin_s, lin_r, hop_s, hop_r, y_s, y_r,
    ) = refs[19:]
    half = heads // 2
    span = SPAN * tok
    width = span + tok
    me = lax.axis_index("ctx")
    hd = lax.axis_index("head")
    k = lax.rem(me, 2)
    first = k == 0
    par = me + 1 - 2 * k
    nxt = lax.rem(me + 2, n_ctx)
    prv = lax.rem(me + n_ctx - 2, n_ctx)
    inv_root = 1.0 / math.sqrt(size)

    def window(ref, h, part):
        return ref[h, pl.ds(k, SPAN + 1), part].reshape(width, size)

    mine = pl.ds(2 * k, half)
    theirs = pl.ds(2 * (1 - k), half)

    copies = {}

    def remote(name, src, dst, send, recv, where):
        copies[name] = pltpu.make_async_remote_copy(
            src_ref=src, dst_ref=dst, send_sem=send, recv_sem=recv,
            device_id=where, device_id_type=MESH,
        )

    barrier = pltpu.get_barrier_semaphore()
    before = [lax.rem(me + n_ctx - step, n_ctx) for step in range(1, SPAN + 1)]
    after = [lax.rem(me + step, n_ctx) for step in range(1, SPAN + 1)]
    for other in before + after:
        pl.semaphore_signal(barrier, inc=1, device_id=(other, hd), device_id_type=MESH)
    peers = [(me, lax.rem(hd + step, n_head)) for step in range(1, n_head)]
    for peer in peers:
        pl.semaphore_signal(barrier, inc=1, device_id=peer, device_id_type=MESH)

    loads = [pltpu.make_async_copy(ins[i], raw.at[i], in_sem.at[i]) for i in range(8)]
    small = [
        pltpu.make_async_copy(ds_in, dsv, small_sem.at[0]),
        pltpu.make_async_copy(ld_in, ldv, small_sem.at[1]),
        pltpu.make_async_copy(ng_in, ngv, small_sem.at[2]),
    ]
    for copy in small:
        copy.start()
    for i in (LK, LV, SK, SV):
        loads[i].start()
    for i in (SQ, SC, LQ, LC):
        loads[i].start()

    for h in range(heads):
        whole = kv.at[h]

        def block(slot):
            return whole.at[slot]

        sems = [(fwd_s.at[kind], fwd_r.at[kind, h]) for kind in range(4)]
        if h > 0:
            remote(("near", h), block(4 + k), block(2 + k), *sems[0], (nxt, hd))
        else:
            for part in range(2):
                remote(
                    ("near", h, part), block(4 + k).at[part], block(2 + k).at[part],
                    fwd_s.at[0], (fwd_r.at[0, 0], v_r.at[0])[part], (nxt, hd),
                )
        remote(("far", h), block(2 + k), block(k), *sems[1], (nxt, hd))
        remote(("core", h), block(4 - k), block(4 - k), *sems[2], (par, hd))
        remote(("core2", h), block(2 - k), block(2 - k), *sems[3], (par, hd))
        queries = qd.at[h]

        def qblock(slot):
            return queries.at[slot]

        sems = [(bwd_s.at[kind], bwd_r.at[kind, h]) for kind in range(4)]
        remote(("qnear", h), qblock(k), qblock(2 + k), *sems[0], (prv, hd))
        remote(("qfar", h), qblock(2 + k), qblock(4 + k), *sems[1], (prv, hd))
        remote(("qcore", h), qblock(2 - k), qblock(2 - k), *sems[2], (par, hd))
        remote(("qcore2", h), qblock(4 - k), qblock(4 - k), *sems[3], (par, hd))
        for i in range(SPAN):
            remote(
                ("stats", h, i), stats.at[h, 0], stats.at[h, i + 1],
                st_s.at[0], st_r.at[h], (before[i], hd),
            )
    lin = [
        ("closing", cl.at[theirs], clr, par),
        ("pass", ptile.at[0], ptile.at[1], par),
        ("state", isend, st.at[mine], par),
        ("pulled", pu.at[theirs], pur, par),
        ("back", osend, back.at[mine], par),
    ]
    for i, (name, src, dst, where) in enumerate(lin):
        remote(name, src, dst, lin_s.at[i], lin_r.at[i], (where, hd))
    for j in range(half):
        hops = [
            ("s", ssend, snear, nxt), ("t", tsend, sfar, nxt),
            ("r", rsend, rnear, prv), ("q", qsend, rfar, prv),
        ]
        for i, (name, src, dst, where) in enumerate(hops):
            remote(
                (name, j), src.at[j], dst.at[j], hop_s.at[i], hop_r.at[i, j], (where, hd)
            )
    for step, peer in enumerate(peers):
        remote(("sums", step), ysend, yrecv.at[step], y_s.at[0], y_r.at[0], peer)

    def all_of(name, src, dst, send, recv):
        remote(name, src, dst, send, recv, (par, hd))

    for kind, (src, dst) in enumerate(((4 + k, 2 + k), (2 + k, k), (4 - k, 4 - k), (2 - k, 2 - k))):
        all_of(("all", kind), kv.at[:, src], kv.at[:, dst], fwd_s.at[kind], fwd_r.at[kind, 0])
    for kind, (src, dst) in enumerate(((k, 2 + k), (2 + k, 4 + k), (2 - k, 2 - k), (4 - k, 4 - k))):
        all_of(("all", 4 + kind), qd.at[:, src], qd.at[:, dst], bwd_s.at[kind], bwd_r.at[kind, 0])
    later = pl.ds(1, SPAN)
    all_of(("all", 8), stats.at[:, later], stats.at[:, later], st_s.at[0], st_r.at[0])
    for h in range(heads):
        all_of(("figures", h), stats.at[h, later], stats.at[h, later], st_s.at[0], st_r.at[h])
    others = yrecv.at[pl.ds(0, n_head - 1)]
    all_of(("all", 9), others, others, y_s.at[0], y_r.at[0])
    for i, (src, dst) in enumerate(
        ((ssend, snear), (tsend, sfar), (rsend, rnear), (qsend, rfar))
    ):
        all_of(("all", 10 + i), src, dst, hop_s.at[i], hop_r.at[i, 0])

    def head_of(i, h):
        return stage[i, pl.ds(h, tok, stride=heads), :]

    def unpack(i, place):
        loads[i].wait()
        stage[i] = raw[i].astype(F32)
        for h in range(heads):
            if place is not None:
                hb[place, h] = head_of(i, h).astype(BF16)

    def put(place, h, value):
        ostage[place, pl.ds(h, tok, stride=heads), :] = value

    def finish(place):
        outs[place][...] = ostage[place].astype(BF16)

    def pass_rows(j):
        own = ptile[0, pl.ds(2 * k + j, 1), :]
        other = ptile[1, pl.ds(2 * k + j, 1), :]
        return jnp.where(first, own, other), jnp.where(first, other, own)

    def load_kv():
        for i, part in ((SK, 0), (SV, 1)):
            loads[i].wait()
            stage[i] = raw[i].astype(F32)
            for h in range(heads):
                kv[h, 4 + k, part] = head_of(i, h).astype(BF16)

    def load_qd():
        for i, part in ((SQ, 0), (SC, 1)):
            loads[i].wait()
            stage[i] = raw[i].astype(F32)
            for h in range(heads):
                qd[h, k, part] = head_of(i, h).astype(BF16)

    def send_qd(h):
        copies["qnear", h].start()

    def qrelay(h):
        copies["qnear", h].wait_recv()
        copies["qfar", h].start()
        copies["qcore", h].start()

    def qrelay_core(h):
        copies["qfar", h].wait_recv()
        copies["qcore2", h].start()

    def enter_kernel():
        pl.semaphore_wait(barrier, 2 * SPAN + n_head - 1)

    def send_own(h):
        copies["near", h].start()

    def send_first(part):
        copies["near", 0, part].start()

    def relay(h):
        if h > 0:
            copies["near", h].wait_recv()
        else:
            copies["near", 0, 0].wait_recv()
            copies["near", 0, 1].wait_recv()
        copies["far", h].start()
        copies["core", h].start()

    def relay_core(h):
        copies["far", h].wait_recv()
        copies["core2", h].start()

    def soft(h):
        copies["core", h].wait_recv()
        copies["core2", h].wait_recv()
        query, cot = qd[h, k, 0], qd[h, k, 1]
        keys, values = window(kv, h, 0), window(kv, h, 1)
        logits = dot_nt(query, keys) * inv_root + bias[...]
        top = jnp.max(logits, axis=1, keepdims=True)
        expo = jnp.exp(logits - top)
        total = jnp.sum(expo, axis=1, keepdims=True)
        inverse = 1.0 / total
        out = (dot_nn(expo.astype(BF16), values) * inverse).astype(BF16).astype(F32)
        put(O_SOFT, h, out)
        delta = jnp.sum(cot.astype(F32) * out, axis=1, keepdims=True)
        lane = lax.broadcasted_iota(jnp.int32, (tok, tok), 1)
        figures = jnp.where(lane == 0, top + jnp.log(total), jnp.where(lane == 1, delta, mask[1]))
        stats[h, 0] = jnp.transpose(figures)[:8, :]
        for i in range(SPAN):
            copies["stats", h, i].start()
        slopes = inv_root * (expo * inverse) * (dot_nt(cot, values) - delta)
        put(O_SQ, h, dot_nn(slopes.astype(BF16), keys))

    def soft_grad(h):
        copies["qcore", h].wait_recv()
        copies["qcore2", h].wait_recv()
        if h > 0:
            copies["figures", h].wait_recv()
        keys, values = kv[h, 4 + k, 0], kv[h, 4 + k, 1]
        queries, cots = window(qd, h, 0), window(qd, h, 1)
        wide = [
            jnp.concatenate([stats[h, i, row : row + 1, :] for i in range(SPAN + 1)], axis=1)
            for row in range(2)
        ]
        logits = dot_nt(keys, queries) * inv_root + bias_t[...]
        probs = jnp.exp(logits - wide[0])
        put(O_SV, h, dot_nn(probs.astype(BF16), cots))
        slopes = inv_root * probs * (dot_nt(values, cots) - wide[1])
        put(O_SK, h, dot_nn(slopes.astype(BF16), queries))

    def later_mask():
        copies["figures", 0].wait_recv()
        k_index = lax.broadcasted_iota(jnp.int32, (tok, width), 0)
        q_index = lax.broadcasted_iota(jnp.int32, (tok, width), 1)
        starts = jnp.concatenate([stats[0, i, 2:3, :] for i in range(SPAN + 1)], axis=1)
        position = k_index.astype(F32) + (me * tok).astype(F32)
        inside = q_index < (n_ctx - me) * tok
        allowed = (k_index <= q_index) & (position >= starts) & inside
        bias_t[...] = jnp.where(allowed, 0.0, MASKED)

    def decays():
        for copy in small:
            copy.wait()
        t_pos = lax.broadcasted_iota(jnp.int32, (tok, tok), 0)
        s_pos = lax.broadcasted_iota(jnp.int32, (tok, tok), 1)
        first_row = (me * tok).astype(F32)
        ds_row = jnp.broadcast_to(dsv[...].astype(F32), (tok, tok))
        ds_col = jnp.transpose(ds_row)
        mask[0] = jnp.where((ds_row == ds_col) & (s_pos <= t_pos), 1.0, 0.0)
        mask[1] = ds_col
        ds_last = jnp.broadcast_to(ds_row[:, tok - 1 :], (tok, tok))
        triangle = jnp.where(t_pos <= s_pos, 1.0, 0.0).astype(F32)
        logs = jnp.concatenate([ldv[...], jnp.zeros((8 - heads, tok), F32)], axis=0)
        cumulative = lax.dot_general(
            logs, triangle, (((1,), (0,)), ((), ())),
            precision=lax.Precision.HIGHEST, preferred_element_type=F32,
        )
        for h in range(heads):
            cum_row = jnp.broadcast_to(cumulative[h : h + 1, :], (tok, tok))
            cum_col = jnp.transpose(cum_row)
            gap = jnp.exp(jnp.minimum(cum_col - cum_row, 0.0))
            within[h] = jnp.where(mask[0] > 0.0, gap, 0.0)
            enter[h] = jnp.where(ds_col < first_row, jnp.exp(cum_col), 0.0)
            cum_last = jnp.broadcast_to(cum_row[:, tok - 1 :], (tok, tok))
            leave[h] = jnp.where(ds_col == ds_last, jnp.exp(cum_last - cum_col), 0.0)
            ptile[0, h : h + 1, :] = enter[h, tok - 1 :, :]
        ptile[0, heads:, :] = jnp.zeros((8 - heads, size), F32)

    def closing():
        unpack(LK, 1)
        unpack(LV, 2)
        for h in range(heads):
            keyed = (leave[h] * head_of(LK, h)).astype(BF16)
            cl[h] = dot_tn(keyed, hb[2, h])

    def send_closing():
        copies["closing"].start()
        copies["pass"].start()

    def local_lin():
        unpack(LQ, 0)
        for h in range(heads):
            attend[h] = (within[h] * dot_nt(hb[0, h], hb[1, h])).astype(BF16)
            rawo[h] = dot_nn(attend[h], hb[2, h])
        unpack(LC, None)

    def local_soft():
        q_index = lax.broadcasted_iota(jnp.int32, (tok, width), 0) + span
        k_index = lax.broadcasted_iota(jnp.int32, (tok, width), 1)
        starts = jnp.concatenate([mask[1]] * (width // tok), axis=1)
        position = k_index.astype(F32) + (me * tok - span).astype(F32)
        allowed = (k_index <= q_index) & (position >= starts)
        bias[...] = jnp.where(allowed, 0.0, MASKED)

    def state_send():
        copies["pass"].wait_recv()
        pprod[0] = ptile[0] * ptile[1]
        copies["closing"].wait_recv()
        for j in range(half):
            own, other = cl[2 * k + j], clr[j]
            x0, x1 = jnp.where(first, own, other), jnp.where(first, other, own)
            p0, p1 = pass_rows(j)
            x0b[j] = x0
            comb[j] = x1 + p1 * x0
            ssend[j] = comb[j].astype(BF16)
            copies["s", j].start()

    def state_relay():
        for j in range(half):
            copies["s", j].wait_recv()
            both = pprod[0, pl.ds(2 * k + j, 1), :]
            tsend[j] = (comb[j] + both * snear[j].astype(F32)).astype(BF16)
            copies["t", j].start()

    def state_get():
        for j in range(half):
            copies["t", j].wait_recv()
            p0, p1 = pass_rows(j)
            in0 = sfar[j].astype(F32)
            in1 = x0b[j] + p0 * in0
            st[2 * k + j] = jnp.where(first, in0, in1).astype(BF16)
            isend[j] = jnp.where(first, in1, in0).astype(BF16)
        copies["state"].start()

    def lin_raw():
        copies["state"].wait_recv()
        squares = jnp.zeros((tok, size), F32)
        crossed = jnp.zeros((tok, size), F32)
        for h in range(heads):
            value = rawo[h] + enter[h] * dot_nn(hb[0, h], st[h])
            rawo[h] = value
            squares += value * value
            crossed += head_of(LC, h) * ngv[h : h + 1, :] * value
        ysend[0:1, :] = jnp.sum(jnp.transpose(squares), axis=0, keepdims=True)
        ysend[1:2, :] = jnp.sum(jnp.transpose(crossed), axis=0, keepdims=True)
        ysend[2:, :] = jnp.zeros((6, tok), F32)
        for step in range(n_head - 1):
            copies["sums", step].start()

    def lin_norm():
        total = ysend[...]
        copies["all", 9].wait_recv()
        for step in range(n_head - 1):
            total += yrecv[step]
        count = heads * size * n_head
        rscale_row = lax.rsqrt(total[0:1, :] / count + NORM_EPS)
        factor_row = rscale_row * rscale_row * rscale_row * (total[1:2, :] / count)
        rscale = jnp.transpose(jnp.broadcast_to(rscale_row, (tok, tok)))
        factor = jnp.transpose(jnp.broadcast_to(factor_row, (tok, tok)))
        for h in range(heads):
            gain = ngv[h : h + 1, :]
            value = rawo[h]
            put(O_LIN, h, value * rscale * gain)
            grad = (rscale * (head_of(LC, h) * gain) - value * factor).astype(BF16)
            rgrad[h] = grad
            carried = (enter[h] * hb[0, h].astype(F32)).astype(BF16)
            pu[h] = dot_tn(carried, grad)
        copies["pulled"].start()

    def back_send():
        copies["pulled"].wait_recv()
        for j in range(half):
            own, other = pu[2 * k + j], pur[j]
            y0, y1 = jnp.where(first, own, other), jnp.where(first, other, own)
            p0, p1 = pass_rows(j)
            x0b[j] = y1
            comb[j] = y0 + p0 * y1
            rsend[j] = comb[j].astype(BF16)
            copies["r", j].start()

    def back_relay():
        for j in range(half):
            copies["r", j].wait_recv()
            both = pprod[0, pl.ds(2 * k + j, 1), :]
            qsend[j] = (comb[j] + both * rnear[j].astype(F32)).astype(BF16)
            copies["q", j].start()

    def back_get():
        for j in range(half):
            copies["q", j].wait_recv()
            p0, p1 = pass_rows(j)
            out1 = rfar[j].astype(F32)
            out0 = x0b[j] + p1 * out1
            back[2 * k + j] = jnp.where(first, out0, out1).astype(BF16)
            osend[j] = jnp.where(first, out1, out0).astype(BF16)
        copies["back"].start()

    def lin_local_grads():
        for h in range(heads):
            query, key, value, grad = hb[0, h], hb[1, h], hb[2, h], rgrad[h]
            mixed = (within[h] * dot_nt(grad, value)).astype(BF16)
            put(O_LQ, h, dot_nn(mixed, key) + enter[h] * dot_nt(grad, st[h]))
            dkp[h] = dot_tn(mixed, query)
            dvp[h] = dot_tn(attend[h], grad)

    def lin_grads():
        copies["back"].wait_recv()
        for h in range(heads):
            put(O_LK, h, dkp[h] + leave[h] * dot_nt(hb[2, h], back[h]))
            put(O_LV, h, dvp[h] + leave[h] * dot_nn(hb[1, h], back[h]))

    decays()
    closing()
    enter_kernel()
    send_closing()
    load_kv()
    send_first(0)
    load_qd()
    send_qd(0)
    send_qd(1)
    send_qd(2)
    local_lin()
    state_send()
    send_first(1)
    send_own(1)
    send_qd(3)
    local_soft()
    state_relay()
    relay(0)
    send_own(2)
    relay(1)
    send_own(3)
    qrelay(0)
    qrelay(1)
    qrelay(2)
    qrelay(3)
    state_get()
    lin_raw()
    relay_core(0)
    relay(2)
    soft(0)
    qrelay_core(0)
    qrelay_core(1)
    relay_core(1)
    relay(3)
    lin_norm()
    soft(1)
    back_send()
    qrelay_core(2)
    relay_core(2)
    lin_local_grads()
    finish(0)
    finish(1)
    soft(2)
    relay_core(3)
    qrelay_core(3)
    later_mask()
    soft_grad(0)
    back_relay()
    soft(3)
    finish(4)
    finish(5)
    soft_grad(1)
    back_get()
    soft_grad(2)
    lin_grads()
    finish(2)
    finish(3)
    soft_grad(3)
    finish(6)
    finish(7)
    for kind in range(14):
        copies["all", kind].wait_send()
    for name, _, _, _ in lin:
        copies[name].wait_send()


def write_out(*refs):
    copies = [pltpu.make_async_copy(refs[i], refs[8 + i], refs[16].at[i]) for i in range(8)]
    for copy in copies:
        copy.start()
    for copy in copies:
        copy.wait()


def shards(n_ctx, n_head, *args):
    tok, heads, size = args[0].shape
    (lq, lk, lv, ld, ng, lc, sq, sk, sv, sc, ds) = args
    flat = (tok * heads, size)
    big = [a.reshape(flat) for a in (lq, lk, lv, lc, sq, sk, sv, sc)]
    square = (heads, tok, size)
    half = (heads // 2, size, size)
    wide = (heads, SPAN + 2, 2, tok, size)
    vmem = pltpu.VMEM
    dma = pltpu.SemaphoreType.DMA
    any_spec = pl.BlockSpec(memory_space=pl.ANY)
    pair = (heads, 2, tok, size)
    scratch = [
        vmem((8,) + flat, BF16),
        vmem((8,) + flat, F32),
        vmem((3,) + square, BF16),
        vmem(wide, BF16),
        vmem((heads, tok), F32),
        vmem((heads, size), F32),
        vmem((1, tok), jnp.int32),
        vmem((tok, (SPAN + 1) * tok), F32),
        vmem((tok, (SPAN + 1) * tok), F32),
        vmem((2, tok, tok), F32),
        vmem(square, F32),
        vmem(square, F32),
        vmem(square, F32),
        vmem(wide, BF16),
        vmem((heads, SPAN + 1, 8, tok), F32),
        vmem((heads, size, size), F32),
        vmem(half, F32),
        vmem((2, 8, size), F32),
        vmem((1, 8, size), F32),
        vmem(half, F32),
        vmem(half, F32),
        vmem(half, BF16),
        vmem(half, BF16),
        vmem(half, BF16),
        vmem(half, BF16),
        vmem(half, BF16),
        vmem((heads, size, size), BF16),
        vmem((8, tok), F32),
        vmem((n_head, 8, tok), F32),
        vmem((heads, tok, tok), BF16),
        vmem(square, F32),
        vmem(square, BF16),
        vmem((heads, size, size), F32),
        vmem(half, F32),
        vmem(half, BF16),
        vmem(half, BF16),
        vmem(half, BF16),
        vmem(half, BF16),
        vmem(half, BF16),
        vmem((heads, size, size), BF16),
        vmem(square, F32),
        vmem(square, F32),
        vmem((8,) + flat, F32),
        dma((8,)),
        dma((3,)),
        dma((1,)),
        dma((4,)),
        dma((4, heads)),
        dma((4,)),
        dma((4, heads)),
        dma((1,)),
        dma((heads,)),
        dma((5,)),
        dma((5,)),
        dma((4,)),
        dma((4, heads // 2)),
        dma((1,)),
        dma((1,)),
    ]
    results = pl.pallas_call(
        functools.partial(kernel, n_ctx, n_head, heads, tok, size),
        out_shape=[vmem(flat, BF16)] * 8,
        in_specs=[any_spec] * 11,
        out_specs=[pl.BlockSpec(memory_space=pltpu.VMEM)] * 8,
        scratch_shapes=scratch,
        compiler_params=pltpu.CompilerParams(
            collective_id=0, has_side_effects=True, vmem_limit_bytes=48 * 1024 * 1024
        ),
    )(*[pltpu.with_memory_space_constraint(a, pltpu.HBM) for a in (*big, ld, ng, ds.reshape(1, tok))])
    results = pl.pallas_call(
        write_out,
        out_shape=[jax.ShapeDtypeStruct(flat, BF16)] * 8,
        in_specs=[any_spec] * 8,
        out_specs=[any_spec] * 8,
        scratch_shapes=[dma((8,))],
    )(*[pltpu.with_memory_space_constraint(r, pltpu.VMEM) for r in results])
    return tuple(r.reshape(tok, heads, size) for r in results)


def solution(mesh):
    cube = P("ctx", "head", None)
    in_specs = (
        cube, cube, cube, P("head", "ctx"), P("head", None), cube, cube, cube, cube, cube, P("ctx"),
    )
    return jax.shard_map(
        functools.partial(shards, mesh.shape["ctx"], mesh.shape["head"]),
        mesh=mesh, in_specs=in_specs, out_specs=(cube,) * 8, check_vma=False,
    )
```

```python
import functools
import math

import jax
import jax.numpy as jnp
from jax import lax
from jax.experimental import pallas as pl
from jax.experimental.pallas import tpu as pltpu
from jax.sharding import PartitionSpec as P

SPAN = 4
NORM_EPS = 1e-05
MASKED = -1e30
MESH = pl.DeviceIdType.MESH
F32 = jnp.float32
BF16 = jnp.bfloat16

LQ, LK, LV, LC, SQ, SK, SV, SC = range(8)
O_LIN, O_LQ, O_LK, O_LV, O_SOFT, O_SQ, O_SK, O_SV = range(8)


def dot_nn(a, b):
    return lax.dot_general(a, b, (((1,), (0,)), ((), ())), preferred_element_type=F32)


def dot_nt(a, b):
    return lax.dot_general(a, b, (((1,), (1,)), ((), ())), preferred_element_type=F32)


def dot_tn(a, b):
    return lax.dot_general(a, b, (((0,), (0,)), ((), ())), preferred_element_type=F32)


def kernel(n_ctx, n_head, heads, tok, size, *refs):
    ins = refs[:8]
    ld_in, ng_in, ds_in = refs[8:11]
    outs = refs[11:19]
    (
        raw, stage, hb, kv, ldv, ngv, dsv, bias, bias_t, mask, enter, leave, within,
        qd, stats,
        cl, clr, ptile, pprod, x0b, comb, ssend, snear, tsend, sfar, isend, st,
        ysend, yrecv, attend, rawo, rgrad, pu, pur, rsend, rnear, qsend, rfar, osend, back,
        dkp, dvp, ostage,
        in_sem, small_sem, v_r, fwd_s, fwd_r, bwd_s, bwd_r, st_s, st_r, lin_s, lin_r, hop_s, hop_r, y_s, y_r,
    ) = refs[19:]
    half = heads // 2
    span = SPAN * tok
    width = span + tok
    me = lax.axis_index("ctx")
    hd = lax.axis_index("head")
    k = lax.rem(me, 2)
    first = k == 0
    par = me + 1 - 2 * k
    nxt = lax.rem(me + 2, n_ctx)
    prv = lax.rem(me + n_ctx - 2, n_ctx)
    inv_root = 1.0 / math.sqrt(size)

    def window(ref, h, part):
        return ref[h, pl.ds(k, SPAN + 1), part].reshape(width, size)

    mine = pl.ds(2 * k, half)
    theirs = pl.ds(2 * (1 - k), half)

    copies = {}

    def remote(name, src, dst, send, recv, where):
        copies[name] = pltpu.make_async_remote_copy(
            src_ref=src, dst_ref=dst, send_sem=send, recv_sem=recv,
            device_id=where, device_id_type=MESH,
        )

    barrier = pltpu.get_barrier_semaphore()
    before = [lax.rem(me + n_ctx - step, n_ctx) for step in range(1, SPAN + 1)]
    after = [lax.rem(me + step, n_ctx) for step in range(1, SPAN + 1)]
    for other in before + after:
        pl.semaphore_signal(barrier, inc=1, device_id=(other, hd), device_id_type=MESH)
    peers = [(me, lax.rem(hd + step, n_head)) for step in range(1, n_head)]
    for peer in peers:
        pl.semaphore_signal(barrier, inc=1, device_id=peer, device_id_type=MESH)

    loads = [pltpu.make_async_copy(ins[i], raw.at[i], in_sem.at[i]) for i in range(8)]
    small = [
        pltpu.make_async_copy(ds_in, dsv, small_sem.at[0]),
        pltpu.make_async_copy(ld_in, ldv, small_sem.at[1]),
        pltpu.make_async_copy(ng_in, ngv, small_sem.at[2]),
    ]
    for copy in small:
        copy.start()
    for i in (LK, LV, SK, SV):
        loads[i].start()
    for i in (SQ, SC, LQ, LC):
        loads[i].start()

    for h in range(heads):
        whole = kv.at[h]

        def block(slot):
            return whole.at[slot]

        sems = [(fwd_s.at[kind], fwd_r.at[kind, h]) for kind in range(4)]
        if h > 0:
            remote(("near", h), block(4 + k), block(2 + k), *sems[0], (nxt, hd))
        else:
            for part in range(2):
                remote(
                    ("near", h, part), block(4 + k).at[part], block(2 + k).at[part],
                    fwd_s.at[0], (fwd_r.at[0, 0], v_r.at[0])[part], (nxt, hd),
                )
        remote(("far", h), block(2 + k), block(k), *sems[1], (nxt, hd))
        remote(("core", h), block(4 - k), block(4 - k), *sems[2], (par, hd))
        remote(("core2", h), block(2 - k), block(2 - k), *sems[3], (par, hd))
        queries = qd.at[h]

        def qblock(slot):
            return queries.at[slot]

        sems = [(bwd_s.at[kind], bwd_r.at[kind, h]) for kind in range(4)]
        remote(("qnear", h), qblock(k), qblock(2 + k), *sems[0], (prv, hd))
        remote(("qfar", h), qblock(2 + k), qblock(4 + k), *sems[1], (prv, hd))
        remote(("qcore", h), qblock(2 - k), qblock(2 - k), *sems[2], (par, hd))
        remote(("qcore2", h), qblock(4 - k), qblock(4 - k), *sems[3], (par, hd))
        for i in range(SPAN):
            remote(
                ("stats", h, i), stats.at[h, 0], stats.at[h, i + 1],
                st_s.at[0], st_r.at[h], (before[i], hd),
            )
    lin = [
        ("closing", cl.at[theirs], clr, par),
        ("pass", ptile.at[0], ptile.at[1], par),
        ("state", isend, st.at[mine], par),
        ("pulled", pu.at[theirs], pur, par),
        ("back", osend, back.at[mine], par),
    ]
    for i, (name, src, dst, where) in enumerate(lin):
        remote(name, src, dst, lin_s.at[i], lin_r.at[i], (where, hd))
    for j in range(half):
        hops = [
            ("s", ssend, snear, nxt), ("t", tsend, sfar, nxt),
            ("r", rsend, rnear, prv), ("q", qsend, rfar, prv),
        ]
        for i, (name, src, dst, where) in enumerate(hops):
            remote(
                (name, j), src.at[j], dst.at[j], hop_s.at[i], hop_r.at[i, j], (where, hd)
            )
    for step, peer in enumerate(peers):
        remote(("sums", step), ysend, yrecv.at[step], y_s.at[0], y_r.at[0], peer)

    def all_of(name, src, dst, send, recv):
        remote(name, src, dst, send, recv, (par, hd))

    for kind, (src, dst) in enumerate(((4 + k, 2 + k), (2 + k, k), (4 - k, 4 - k), (2 - k, 2 - k))):
        all_of(("all", kind), kv.at[:, src], kv.at[:, dst], fwd_s.at[kind], fwd_r.at[kind, 0])
    for kind, (src, dst) in enumerate(((k, 2 + k), (2 + k, 4 + k), (2 - k, 2 - k), (4 - k, 4 - k))):
        all_of(("all", 4 + kind), qd.at[:, src], qd.at[:, dst], bwd_s.at[kind], bwd_r.at[kind, 0])
    later = pl.ds(1, SPAN)
    all_of(("all", 8), stats.at[:, later], stats.at[:, later], st_s.at[0], st_r.at[0])
    for h in range(heads):
        all_of(("figures", h), stats.at[h, later], stats.at[h, later], st_s.at[0], st_r.at[h])
    others = yrecv.at[pl.ds(0, n_head - 1)]
    all_of(("all", 9), others, others, y_s.at[0], y_r.at[0])
    for i, (src, dst) in enumerate(
        ((ssend, snear), (tsend, sfar), (rsend, rnear), (qsend, rfar))
    ):
        all_of(("all", 10 + i), src, dst, hop_s.at[i], hop_r.at[i, 0])

    def head_of(i, h):
        return stage[i, pl.ds(h, tok, stride=heads), :]

    def unpack(i, place):
        loads[i].wait()
        stage[i] = raw[i].astype(F32)
        for h in range(heads):
            if place is not None:
                hb[place, h] = head_of(i, h).astype(BF16)

    def put(place, h, value):
        ostage[place, pl.ds(h, tok, stride=heads), :] = value

    def finish(place):
        outs[place][...] = ostage[place].astype(BF16)

    def pass_rows(j):
        own = ptile[0, pl.ds(2 * k + j, 1), :]
        other = ptile[1, pl.ds(2 * k + j, 1), :]
        return jnp.where(first, own, other), jnp.where(first, other, own)

    def load_kv():
        for i, part in ((SK, 0), (SV, 1)):
            loads[i].wait()
            stage[i] = raw[i].astype(F32)
            for h in range(heads):
                kv[h, 4 + k, part] = head_of(i, h).astype(BF16)

    def load_qd():
        for i, part in ((SQ, 0), (SC, 1)):
            loads[i].wait()
            stage[i] = raw[i].astype(F32)
            for h in range(heads):
                qd[h, k, part] = head_of(i, h).astype(BF16)

    def send_qd(h):
        copies["qnear", h].start()

    def qrelay(h):
        copies["qnear", h].wait_recv()
        copies["qfar", h].start()
        copies["qcore", h].start()

    def qrelay_core(h):
        copies["qfar", h].wait_recv()
        copies["qcore2", h].start()

    def enter_kernel():
        pl.semaphore_wait(barrier, 2 * SPAN + n_head - 1)

    def send_own(h):
        copies["near", h].start()

    def send_first(part):
        copies["near", 0, part].start()

    def relay(h):
        if h > 0:
            copies["near", h].wait_recv()
        else:
            copies["near", 0, 0].wait_recv()
            copies["near", 0, 1].wait_recv()
        copies["far", h].start()
        copies["core", h].start()

    def relay_core(h):
        copies["far", h].wait_recv()
        copies["core2", h].start()

    def soft(h):
        copies["core", h].wait_recv()
        copies["core2", h].wait_recv()
        query, cot = qd[h, k, 0], qd[h, k, 1]
        keys, values = window(kv, h, 0), window(kv, h, 1)
        logits = dot_nt(query, keys) * inv_root + bias[...]
        top = jnp.max(logits, axis=1, keepdims=True)
        expo = jnp.exp(logits - top)
        total = jnp.sum(expo, axis=1, keepdims=True)
        inverse = 1.0 / total
        out = (dot_nn(expo.astype(BF16), values) * inverse).astype(BF16).astype(F32)
        put(O_SOFT, h, out)
        delta = jnp.sum(cot.astype(F32) * out, axis=1, keepdims=True)
        lane = lax.broadcasted_iota(jnp.int32, (tok, tok), 1)
        figures = jnp.where(lane == 0, top + jnp.log(total), jnp.where(lane == 1, delta, mask[1]))
        stats[h, 0] = jnp.transpose(figures)[:8, :]
        for i in range(SPAN):
            copies["stats", h, i].start()
        slopes = inv_root * (expo * inverse) * (dot_nt(cot, values) - delta)
        put(O_SQ, h, dot_nn(slopes.astype(BF16), keys))

    def soft_grad(h):
        copies["qcore", h].wait_recv()
        copies["qcore2", h].wait_recv()
        if h > 0:
            copies["figures", h].wait_recv()
        keys, values = kv[h, 4 + k, 0], kv[h, 4 + k, 1]
        queries, cots = window(qd, h, 0), window(qd, h, 1)
        wide = [
            jnp.concatenate([stats[h, i, row : row + 1, :] for i in range(SPAN + 1)], axis=1)
            for row in range(2)
        ]
        logits = dot_nt(keys, queries) * inv_root + bias_t[...]
        probs = jnp.exp(logits - wide[0])
        put(O_SV, h, dot_nn(probs.astype(BF16), cots))
        slopes = inv_root * probs * (dot_nt(values, cots) - wide[1])
        put(O_SK, h, dot_nn(slopes.astype(BF16), queries))

    def later_mask():
        copies["figures", 0].wait_recv()
        k_index = lax.broadcasted_iota(jnp.int32, (tok, width), 0)
        q_index = lax.broadcasted_iota(jnp.int32, (tok, width), 1)
        starts = jnp.concatenate([stats[0, i, 2:3, :] for i in range(SPAN + 1)], axis=1)
        position = k_index.astype(F32) + (me * tok).astype(F32)
        inside = q_index < (n_ctx - me) * tok
        allowed = (k_index <= q_index) & (position >= starts) & inside
        bias_t[...] = jnp.where(allowed, 0.0, MASKED)

    def decays():
        for copy in small:
            copy.wait()
        t_pos = lax.broadcasted_iota(jnp.int32, (tok, tok), 0)
        s_pos = lax.broadcasted_iota(jnp.int32, (tok, tok), 1)
        first_row = (me * tok).astype(F32)
        ds_row = jnp.broadcast_to(dsv[...].astype(F32), (tok, tok))
        ds_col = jnp.transpose(ds_row)
        mask[0] = jnp.where((ds_row == ds_col) & (s_pos <= t_pos), 1.0, 0.0)
        mask[1] = ds_col
        ds_last = jnp.broadcast_to(ds_row[:, tok - 1 :], (tok, tok))
        triangle = jnp.where(t_pos <= s_pos, 1.0, 0.0).astype(F32)
        logs = jnp.concatenate([ldv[...], jnp.zeros((8 - heads, tok), F32)], axis=0)
        cumulative = lax.dot_general(
            logs, triangle, (((1,), (0,)), ((), ())),
            precision=lax.Precision.HIGHEST, preferred_element_type=F32,
        )
        for h in range(heads):
            cum_row = jnp.broadcast_to(cumulative[h : h + 1, :], (tok, tok))
            cum_col = jnp.transpose(cum_row)
            gap = jnp.exp(jnp.minimum(cum_col - cum_row, 0.0))
            within[h] = jnp.where(mask[0] > 0.0, gap, 0.0)
            enter[h] = jnp.where(ds_col < first_row, jnp.exp(cum_col), 0.0)
            cum_last = jnp.broadcast_to(cum_row[:, tok - 1 :], (tok, tok))
            leave[h] = jnp.where(ds_col == ds_last, jnp.exp(cum_last - cum_col), 0.0)
            ptile[0, h : h + 1, :] = enter[h, tok - 1 :, :]
        ptile[0, heads:, :] = jnp.zeros((8 - heads, size), F32)

    def closing():
        unpack(LK, 1)
        unpack(LV, 2)
        for h in range(heads):
            keyed = (leave[h] * head_of(LK, h)).astype(BF16)
            cl[h] = dot_tn(keyed, hb[2, h])

    def send_closing():
        copies["closing"].start()
        copies["pass"].start()

    def local_lin():
        unpack(LQ, 0)
        for h in range(heads):
            attend[h] = (within[h] * dot_nt(hb[0, h], hb[1, h])).astype(BF16)
            rawo[h] = dot_nn(attend[h], hb[2, h])
        unpack(LC, None)

    def local_soft():
        q_index = lax.broadcasted_iota(jnp.int32, (tok, width), 0) + span
        k_index = lax.broadcasted_iota(jnp.int32, (tok, width), 1)
        starts = jnp.concatenate([mask[1]] * (width // tok), axis=1)
        position = k_index.astype(F32) + (me * tok - span).astype(F32)
        allowed = (k_index <= q_index) & (position >= starts)
        bias[...] = jnp.where(allowed, 0.0, MASKED)

    def state_send():
        copies["pass"].wait_recv()
        pprod[0] = ptile[0] * ptile[1]
        copies["closing"].wait_recv()
        for j in range(half):
            own, other = cl[2 * k + j], clr[j]
            x0, x1 = jnp.where(first, own, other), jnp.where(first, other, own)
            p0, p1 = pass_rows(j)
            x0b[j] = x0
            comb[j] = x1 + p1 * x0
            ssend[j] = comb[j].astype(BF16)
            copies["s", j].start()

    def state_relay():
        for j in range(half):
            copies["s", j].wait_recv()
            both = pprod[0, pl.ds(2 * k + j, 1), :]
            tsend[j] = (comb[j] + both * snear[j].astype(F32)).astype(BF16)
            copies["t", j].start()

    def state_get():
        for j in range(half):
            copies["t", j].wait_recv()
            p0, p1 = pass_rows(j)
            in0 = sfar[j].astype(F32)
            in1 = x0b[j] + p0 * in0
            st[2 * k + j] = jnp.where(first, in0, in1).astype(BF16)
            isend[j] = jnp.where(first, in1, in0).astype(BF16)
        copies["state"].start()

    def lin_raw():
        copies["state"].wait_recv()
        squares = jnp.zeros((tok, size), F32)
        crossed = jnp.zeros((tok, size), F32)
        for h in range(heads):
            value = rawo[h] + enter[h] * dot_nn(hb[0, h], st[h])
            rawo[h] = value
            squares += value * value
            crossed += head_of(LC, h) * ngv[h : h + 1, :] * value
        ysend[0:1, :] = jnp.sum(jnp.transpose(squares), axis=0, keepdims=True)
        ysend[1:2, :] = jnp.sum(jnp.transpose(crossed), axis=0, keepdims=True)
        for step in range(n_head - 1):
            copies["sums", step].start()

    def lin_norm():
        total = ysend[...]
        copies["all", 9].wait_recv()
        for step in range(n_head - 1):
            total += yrecv[step]
        count = heads * size * n_head
        rscale_row = lax.rsqrt(total[0:1, :] / count + NORM_EPS)
        factor_row = rscale_row * rscale_row * rscale_row * (total[1:2, :] / count)
        rscale = jnp.transpose(jnp.broadcast_to(rscale_row, (tok, tok)))
        factor = jnp.transpose(jnp.broadcast_to(factor_row, (tok, tok)))
        for h in range(heads):
            gain = ngv[h : h + 1, :]
            value = rawo[h]
            put(O_LIN, h, value * rscale * gain)
            grad = (rscale * (head_of(LC, h) * gain) - value * factor).astype(BF16)
            rgrad[h] = grad
            carried = (enter[h] * hb[0, h].astype(F32)).astype(BF16)
            pu[h] = dot_tn(carried, grad)
        copies["pulled"].start()

    def back_send():
        copies["pulled"].wait_recv()
        for j in range(half):
            own, other = pu[2 * k + j], pur[j]
            y0, y1 = jnp.where(first, own, other), jnp.where(first, other, own)
            p0, p1 = pass_rows(j)
            x0b[j] = y1
            comb[j] = y0 + p0 * y1
            rsend[j] = comb[j].astype(BF16)
            copies["r", j].start()

    def back_relay():
        for j in range(half):
            copies["r", j].wait_recv()
            both = pprod[0, pl.ds(2 * k + j, 1), :]
            qsend[j] = (comb[j] + both * rnear[j].astype(F32)).astype(BF16)
            copies["q", j].start()

    def back_get():
        for j in range(half):
            copies["q", j].wait_recv()
            p0, p1 = pass_rows(j)
            out1 = rfar[j].astype(F32)
            out0 = x0b[j] + p1 * out1
            back[2 * k + j] = jnp.where(first, out0, out1).astype(BF16)
            osend[j] = jnp.where(first, out1, out0).astype(BF16)
        copies["back"].start()

    def lin_local_grads():
        for h in range(heads):
            query, key, value, grad = hb[0, h], hb[1, h], hb[2, h], rgrad[h]
            mixed = (within[h] * dot_nt(grad, value)).astype(BF16)
            put(O_LQ, h, dot_nn(mixed, key) + enter[h] * dot_nt(grad, st[h]))
            dkp[h] = dot_tn(mixed, query)
            dvp[h] = dot_tn(attend[h], grad)

    def lin_grads():
        copies["back"].wait_recv()
        for h in range(heads):
            put(O_LK, h, dkp[h] + leave[h] * dot_nt(hb[2, h], back[h]))
            put(O_LV, h, dvp[h] + leave[h] * dot_nn(hb[1, h], back[h]))

    decays()
    closing()
    enter_kernel()
    send_closing()
    load_kv()
    send_first(0)
    load_qd()
    send_qd(0)
    send_qd(1)
    send_qd(2)
    local_lin()
    state_send()
    send_first(1)
    send_own(1)
    send_qd(3)
    local_soft()
    state_relay()
    relay(0)
    send_own(2)
    relay(1)
    send_own(3)
    qrelay(0)
    qrelay(1)
    qrelay(2)
    qrelay(3)
    state_get()
    lin_raw()
    relay_core(0)
    relay(2)
    soft(0)
    qrelay_core(0)
    qrelay_core(1)
    relay_core(1)
    relay(3)
    lin_norm()
    soft(1)
    back_send()
    qrelay_core(2)
    relay_core(2)
    lin_local_grads()
    finish(0)
    finish(1)
    soft(2)
    relay_core(3)
    qrelay_core(3)
    later_mask()
    soft_grad(0)
    back_relay()
    soft(3)
    finish(4)
    finish(5)
    soft_grad(1)
    soft_grad(2)
    back_get()
    soft_grad(3)
    lin_grads()
    finish(2)
    finish(3)
    finish(6)
    finish(7)
    for kind in range(14):
        copies["all", kind].wait_send()
    for name, _, _, _ in lin:
        copies[name].wait_send()


def write_out(*refs):
    copies = [pltpu.make_async_copy(refs[i], refs[8 + i], refs[16].at[i]) for i in range(8)]
    for copy in copies:
        copy.start()
    for copy in copies:
        copy.wait()


def shards(n_ctx, n_head, *args):
    tok, heads, size = args[0].shape
    (lq, lk, lv, ld, ng, lc, sq, sk, sv, sc, ds) = args
    flat = (tok * heads, size)
    big = [a.reshape(flat) for a in (lq, lk, lv, lc, sq, sk, sv, sc)]
    square = (heads, tok, size)
    half = (heads // 2, size, size)
    wide = (heads, SPAN + 2, 2, tok, size)
    vmem = pltpu.VMEM
    dma = pltpu.SemaphoreType.DMA
    any_spec = pl.BlockSpec(memory_space=pl.ANY)
    pair = (heads, 2, tok, size)
    scratch = [
        vmem((8,) + flat, BF16),
        vmem((8,) + flat, F32),
        vmem((3,) + square, BF16),
        vmem(wide, BF16),
        vmem((heads, tok), F32),
        vmem((heads, size), F32),
        vmem((1, tok), jnp.int32),
        vmem((tok, (SPAN + 1) * tok), F32),
        vmem((tok, (SPAN + 1) * tok), F32),
        vmem((2, tok, tok), F32),
        vmem(square, F32),
        vmem(square, F32),
        vmem(square, F32),
        vmem(wide, BF16),
        vmem((heads, SPAN + 1, 8, tok), F32),
        vmem((heads, size, size), F32),
        vmem(half, F32),
        vmem((2, 8, size), F32),
        vmem((1, 8, size), F32),
        vmem(half, F32),
        vmem(half, F32),
        vmem(half, BF16),
        vmem(half, BF16),
        vmem(half, BF16),
        vmem(half, BF16),
        vmem(half, BF16),
        vmem((heads, size, size), BF16),
        vmem((2, tok), F32),
        vmem((n_head, 2, tok), F32),
        vmem((heads, tok, tok), BF16),
        vmem(square, F32),
        vmem(square, BF16),
        vmem((heads, size, size), F32),
        vmem(half, F32),
        vmem(half, BF16),
        vmem(half, BF16),
        vmem(half, BF16),
        vmem(half, BF16),
        vmem(half, BF16),
        vmem((heads, size, size), BF16),
        vmem(square, F32),
        vmem(square, F32),
        vmem((8,) + flat, F32),
        dma((8,)),
        dma((3,)),
        dma((1,)),
        dma((4,)),
        dma((4, heads)),
        dma((4,)),
        dma((4, heads)),
        dma((1,)),
        dma((heads,)),
        dma((5,)),
        dma((5,)),
        dma((4,)),
        dma((4, heads // 2)),
        dma((1,)),
        dma((1,)),
    ]
    results = pl.pallas_call(
        functools.partial(kernel, n_ctx, n_head, heads, tok, size),
        out_shape=[vmem(flat, BF16)] * 8,
        in_specs=[any_spec] * 11,
        out_specs=[pl.BlockSpec(memory_space=pltpu.VMEM)] * 8,
        scratch_shapes=scratch,
        compiler_params=pltpu.CompilerParams(
            collective_id=0, has_side_effects=True, vmem_limit_bytes=48 * 1024 * 1024
        ),
    )(*[pltpu.with_memory_space_constraint(a, pltpu.HBM) for a in (*big, ld, ng, ds.reshape(1, tok))])
    results = pl.pallas_call(
        write_out,
        out_shape=[jax.ShapeDtypeStruct(flat, BF16)] * 8,
        in_specs=[any_spec] * 8,
        out_specs=[any_spec] * 8,
        scratch_shapes=[dma((8,))],
    )(*[pltpu.with_memory_space_constraint(r, pltpu.VMEM) for r in results])
    return tuple(r.reshape(tok, heads, size) for r in results)


def solution(mesh):
    cube = P("ctx", "head", None)
    in_specs = (
        cube, cube, cube, P("head", "ctx"), P("head", None), cube, cube, cube, cube, cube, P("ctx"),
    )
    return jax.shard_map(
        functools.partial(shards, mesh.shape["ctx"], mesh.shape["head"]),
        mesh=mesh, in_specs=in_specs, out_specs=(cube,) * 8, check_vma=False,
    )
```

```python
import functools
import math

import jax
import jax.numpy as jnp
from jax import lax
from jax.experimental import pallas as pl
from jax.experimental.pallas import tpu as pltpu
from jax.sharding import PartitionSpec as P

SPAN = 4
NORM_EPS = 1e-05
MASKED = -1e30
MESH = pl.DeviceIdType.MESH
F32 = jnp.float32
BF16 = jnp.bfloat16

LQ, LK, LV, LC, SQ, SK, SV, SC = range(8)
O_LIN, O_LQ, O_LK, O_LV, O_SOFT, O_SQ, O_SK, O_SV = range(8)


def dot_nn(a, b):
    return lax.dot_general(a, b, (((1,), (0,)), ((), ())), preferred_element_type=F32)


def dot_nt(a, b):
    return lax.dot_general(a, b, (((1,), (1,)), ((), ())), preferred_element_type=F32)


def dot_tn(a, b):
    return lax.dot_general(a, b, (((0,), (0,)), ((), ())), preferred_element_type=F32)


def kernel(n_ctx, n_head, heads, tok, size, *refs):
    ins = refs[:8]
    ld_in, ng_in, ds_in = refs[8:11]
    outs = refs[11:19]
    (
        raw, stage, hb, kv, ldv, ngv, dsv, bias, bias_t, mask, enter, leave, within,
        qd, stats,
        cl, clr, ptile, pprod, x0b, comb, ssend, snear, tsend, sfar, isend, st,
        ysend, yrecv, attend, rawo, rgrad, pu, pur, rsend, rnear, qsend, rfar, osend, back,
        dkp, dvp, ostage,
        in_sem, small_sem, v_r, fwd_s, fwd_r, bwd_s, bwd_r, st_s, st_r, lin_s, lin_r, hop_s, hop_r, y_s, y_r,
    ) = refs[19:]
    half = heads // 2
    span = SPAN * tok
    width = span + tok
    me = lax.axis_index("ctx")
    hd = lax.axis_index("head")
    k = lax.rem(me, 2)
    first = k == 0
    par = me + 1 - 2 * k
    nxt = lax.rem(me + 2, n_ctx)
    prv = lax.rem(me + n_ctx - 2, n_ctx)
    inv_root = 1.0 / math.sqrt(size)

    def window(ref, h, part):
        return ref[h, pl.ds(k, SPAN + 1), part].reshape(width, size)

    mine = pl.ds(2 * k, half)
    theirs = pl.ds(2 * (1 - k), half)

    copies = {}

    def remote(name, src, dst, send, recv, where):
        copies[name] = pltpu.make_async_remote_copy(
            src_ref=src, dst_ref=dst, send_sem=send, recv_sem=recv,
            device_id=where, device_id_type=MESH,
        )

    barrier = pltpu.get_barrier_semaphore()
    before = [lax.rem(me + n_ctx - step, n_ctx) for step in range(1, SPAN + 1)]
    after = [lax.rem(me + step, n_ctx) for step in range(1, SPAN + 1)]
    for other in before + after:
        pl.semaphore_signal(barrier, inc=1, device_id=(other, hd), device_id_type=MESH)
    peers = [(me, lax.rem(hd + step, n_head)) for step in range(1, n_head)]
    for peer in peers:
        pl.semaphore_signal(barrier, inc=1, device_id=peer, device_id_type=MESH)

    loads = [pltpu.make_async_copy(ins[i], raw.at[i], in_sem.at[i]) for i in range(8)]
    small = [
        pltpu.make_async_copy(ds_in, dsv, small_sem.at[0]),
        pltpu.make_async_copy(ld_in, ldv, small_sem.at[1]),
        pltpu.make_async_copy(ng_in, ngv, small_sem.at[2]),
    ]
    for copy in small:
        copy.start()
    for i in (LK, LV, SK, SV):
        loads[i].start()
    for i in (SQ, SC, LQ, LC):
        loads[i].start()

    for h in range(heads):
        whole = kv.at[h]

        def block(slot):
            return whole.at[slot]

        sems = [(fwd_s.at[kind], fwd_r.at[kind, h]) for kind in range(4)]
        if h > 0:
            remote(("near", h), block(4 + k), block(2 + k), *sems[0], (nxt, hd))
        else:
            for part in range(2):
                remote(
                    ("near", h, part), block(4 + k).at[part], block(2 + k).at[part],
                    fwd_s.at[0], (fwd_r.at[0, 0], v_r.at[0])[part], (nxt, hd),
                )
        remote(("far", h), block(2 + k), block(k), *sems[1], (nxt, hd))
        remote(("core", h), block(4 - k), block(4 - k), *sems[2], (par, hd))
        remote(("core2", h), block(2 - k), block(2 - k), *sems[3], (par, hd))
        queries = qd.at[h]

        def qblock(slot):
            return queries.at[slot]

        sems = [(bwd_s.at[kind], bwd_r.at[kind, h]) for kind in range(4)]
        remote(("qnear", h), qblock(k), qblock(2 + k), *sems[0], (prv, hd))
        remote(("qfar", h), qblock(2 + k), qblock(4 + k), *sems[1], (prv, hd))
        remote(("qcore", h), qblock(2 - k), qblock(2 - k), *sems[2], (par, hd))
        remote(("qcore2", h), qblock(4 - k), qblock(4 - k), *sems[3], (par, hd))
        for i in range(SPAN):
            remote(
                ("stats", h, i), stats.at[h, 0], stats.at[h, i + 1],
                st_s.at[0], st_r.at[h], (before[i], hd),
            )
    lin = [
        ("closing", cl.at[theirs], clr, par),
        ("pass", ptile.at[0], ptile.at[1], par),
        ("state", isend, st.at[mine], par),
        ("pulled", pu.at[theirs], pur, par),
        ("back", osend, back.at[mine], par),
    ]
    for i, (name, src, dst, where) in enumerate(lin):
        remote(name, src, dst, lin_s.at[i], lin_r.at[i], (where, hd))
    for j in range(half):
        hops = [
            ("s", ssend, snear, nxt), ("t", tsend, sfar, nxt),
            ("r", rsend, rnear, prv), ("q", qsend, rfar, prv),
        ]
        for i, (name, src, dst, where) in enumerate(hops):
            remote(
                (name, j), src.at[j], dst.at[j], hop_s.at[i], hop_r.at[i, j], (where, hd)
            )
    for step, peer in enumerate(peers):
        remote(("sums", step), ysend, yrecv.at[step], y_s.at[0], y_r.at[0], peer)

    def all_of(name, src, dst, send, recv):
        remote(name, src, dst, send, recv, (par, hd))

    for kind, (src, dst) in enumerate(((4 + k, 2 + k), (2 + k, k), (4 - k, 4 - k), (2 - k, 2 - k))):
        all_of(("all", kind), kv.at[:, src], kv.at[:, dst], fwd_s.at[kind], fwd_r.at[kind, 0])
    for kind, (src, dst) in enumerate(((k, 2 + k), (2 + k, 4 + k), (2 - k, 2 - k), (4 - k, 4 - k))):
        all_of(("all", 4 + kind), qd.at[:, src], qd.at[:, dst], bwd_s.at[kind], bwd_r.at[kind, 0])
    later = pl.ds(1, SPAN)
    all_of(("all", 8), stats.at[:, later], stats.at[:, later], st_s.at[0], st_r.at[0])
    for h in range(heads):
        all_of(("figures", h), stats.at[h, later], stats.at[h, later], st_s.at[0], st_r.at[h])
    others = yrecv.at[pl.ds(0, n_head - 1)]
    all_of(("all", 9), others, others, y_s.at[0], y_r.at[0])
    for i, (src, dst) in enumerate(
        ((ssend, snear), (tsend, sfar), (rsend, rnear), (qsend, rfar))
    ):
        all_of(("all", 10 + i), src, dst, hop_s.at[i], hop_r.at[i, 0])

    def head_of(i, h):
        return stage[i, pl.ds(h, tok, stride=heads), :]

    def unpack(i, place):
        loads[i].wait()
        stage[i] = raw[i].astype(F32)
        for h in range(heads):
            if place is not None:
                hb[place, h] = head_of(i, h).astype(BF16)

    def put(place, h, value):
        ostage[place, pl.ds(h, tok, stride=heads), :] = value

    def finish(place):
        outs[place][...] = ostage[place].astype(BF16)

    def pass_rows(j):
        own = ptile[0, pl.ds(2 * k + j, 1), :]
        other = ptile[1, pl.ds(2 * k + j, 1), :]
        return jnp.where(first, own, other), jnp.where(first, other, own)

    def load_kv():
        for i, part in ((SK, 0), (SV, 1)):
            loads[i].wait()
            stage[i] = raw[i].astype(F32)
            for h in range(heads):
                kv[h, 4 + k, part] = head_of(i, h).astype(BF16)

    def load_qd():
        for i, part in ((SQ, 0), (SC, 1)):
            loads[i].wait()
            stage[i] = raw[i].astype(F32)
            for h in range(heads):
                qd[h, k, part] = head_of(i, h).astype(BF16)

    def send_qd(h):
        copies["qnear", h].start()

    def qrelay(h):
        copies["qnear", h].wait_recv()
        copies["qfar", h].start()
        copies["qcore", h].start()

    def qrelay_core(h):
        copies["qfar", h].wait_recv()
        copies["qcore2", h].start()

    def enter_kernel():
        pl.semaphore_wait(barrier, 2 * SPAN + n_head - 1)

    def send_own(h):
        copies["near", h].start()

    def send_first(part):
        copies["near", 0, part].start()

    def relay(h):
        if h > 0:
            copies["near", h].wait_recv()
        else:
            copies["near", 0, 0].wait_recv()
            copies["near", 0, 1].wait_recv()
        copies["far", h].start()
        copies["core", h].start()

    def relay_core(h):
        copies["far", h].wait_recv()
        copies["core2", h].start()

    def soft(h):
        copies["core", h].wait_recv()
        copies["core2", h].wait_recv()
        query, cot = qd[h, k, 0], qd[h, k, 1]
        keys, values = window(kv, h, 0), window(kv, h, 1)
        logits = dot_nt(query, keys) * inv_root + bias[...]
        top = jnp.max(logits, axis=1, keepdims=True)
        expo = jnp.exp(logits - top)
        total = jnp.sum(expo, axis=1, keepdims=True)
        inverse = 1.0 / total
        out = (dot_nn(expo.astype(BF16), values) * inverse).astype(BF16).astype(F32)
        put(O_SOFT, h, out)
        delta = jnp.sum(cot.astype(F32) * out, axis=1, keepdims=True)
        lane = lax.broadcasted_iota(jnp.int32, (tok, tok), 1)
        figures = jnp.where(lane == 0, top + jnp.log(total), jnp.where(lane == 1, delta, mask[1]))
        stats[h, 0] = jnp.transpose(figures)[:4, :]
        for i in range(SPAN):
            copies["stats", h, i].start()
        slopes = inv_root * (expo * inverse) * (dot_nt(cot, values) - delta)
        put(O_SQ, h, dot_nn(slopes.astype(BF16), keys))

    def soft_grad(h):
        copies["qcore", h].wait_recv()
        copies["qcore2", h].wait_recv()
        if h > 0:
            copies["figures", h].wait_recv()
        keys, values = kv[h, 4 + k, 0], kv[h, 4 + k, 1]
        queries, cots = window(qd, h, 0), window(qd, h, 1)
        wide = [
            jnp.concatenate([stats[h, i, row : row + 1, :] for i in range(SPAN + 1)], axis=1)
            for row in range(2)
        ]
        logits = dot_nt(keys, queries) * inv_root + bias_t[...]
        probs = jnp.exp(logits - wide[0])
        put(O_SV, h, dot_nn(probs.astype(BF16), cots))
        slopes = inv_root * probs * (dot_nt(values, cots) - wide[1])
        put(O_SK, h, dot_nn(slopes.astype(BF16), queries))

    def later_mask():
        copies["figures", 0].wait_recv()
        k_index = lax.broadcasted_iota(jnp.int32, (tok, width), 0)
        q_index = lax.broadcasted_iota(jnp.int32, (tok, width), 1)
        starts = jnp.concatenate([stats[0, i, 2:3, :] for i in range(SPAN + 1)], axis=1)
        position = k_index.astype(F32) + (me * tok).astype(F32)
        inside = q_index < (n_ctx - me) * tok
        allowed = (k_index <= q_index) & (position >= starts) & inside
        bias_t[...] = jnp.where(allowed, 0.0, MASKED)

    def decays():
        for copy in small:
            copy.wait()
        t_pos = lax.broadcasted_iota(jnp.int32, (tok, tok), 0)
        s_pos = lax.broadcasted_iota(jnp.int32, (tok, tok), 1)
        first_row = (me * tok).astype(F32)
        ds_row = jnp.broadcast_to(dsv[...].astype(F32), (tok, tok))
        ds_col = jnp.transpose(ds_row)
        mask[0] = jnp.where((ds_row == ds_col) & (s_pos <= t_pos), 1.0, 0.0)
        mask[1] = ds_col
        ds_last = jnp.broadcast_to(ds_row[:, tok - 1 :], (tok, tok))
        triangle = jnp.where(t_pos <= s_pos, 1.0, 0.0).astype(F32)
        logs = jnp.concatenate([ldv[...], jnp.zeros((8 - heads, tok), F32)], axis=0)
        cumulative = lax.dot_general(
            logs, triangle, (((1,), (0,)), ((), ())),
            precision=lax.Precision.HIGHEST, preferred_element_type=F32,
        )
        for h in range(heads):
            cum_row = jnp.broadcast_to(cumulative[h : h + 1, :], (tok, tok))
            cum_col = jnp.transpose(cum_row)
            gap = jnp.exp(jnp.minimum(cum_col - cum_row, 0.0))
            within[h] = jnp.where(mask[0] > 0.0, gap, 0.0)
            enter[h] = jnp.where(ds_col < first_row, jnp.exp(cum_col), 0.0)
            cum_last = jnp.broadcast_to(cum_row[:, tok - 1 :], (tok, tok))
            leave[h] = jnp.where(ds_col == ds_last, jnp.exp(cum_last - cum_col), 0.0)
            ptile[0, h : h + 1, :] = enter[h, tok - 1 :, :]
        ptile[0, heads:, :] = jnp.zeros((8 - heads, size), F32)

    def closing():
        unpack(LK, 1)
        unpack(LV, 2)
        for h in range(heads):
            keyed = (leave[h] * head_of(LK, h)).astype(BF16)
            cl[h] = dot_tn(keyed, hb[2, h])

    def send_closing():
        copies["closing"].start()
        copies["pass"].start()

    def local_lin():
        unpack(LQ, 0)
        for h in range(heads):
            attend[h] = (within[h] * dot_nt(hb[0, h], hb[1, h])).astype(BF16)
            rawo[h] = dot_nn(attend[h], hb[2, h])
        unpack(LC, None)

    def local_soft():
        q_index = lax.broadcasted_iota(jnp.int32, (tok, width), 0) + span
        k_index = lax.broadcasted_iota(jnp.int32, (tok, width), 1)
        starts = jnp.concatenate([mask[1]] * (width // tok), axis=1)
        position = k_index.astype(F32) + (me * tok - span).astype(F32)
        allowed = (k_index <= q_index) & (position >= starts)
        bias[...] = jnp.where(allowed, 0.0, MASKED)

    def state_send():
        copies["pass"].wait_recv()
        pprod[0] = ptile[0] * ptile[1]
        copies["closing"].wait_recv()
        for j in range(half):
            own, other = cl[2 * k + j], clr[j]
            x0, x1 = jnp.where(first, own, other), jnp.where(first, other, own)
            p0, p1 = pass_rows(j)
            x0b[j] = x0
            comb[j] = x1 + p1 * x0
            ssend[j] = comb[j].astype(BF16)
            copies["s", j].start()

    def state_relay():
        for j in range(half):
            copies["s", j].wait_recv()
            both = pprod[0, pl.ds(2 * k + j, 1), :]
            tsend[j] = (comb[j] + both * snear[j].astype(F32)).astype(BF16)
            copies["t", j].start()

    def state_get():
        for j in range(half):
            copies["t", j].wait_recv()
            p0, p1 = pass_rows(j)
            in0 = sfar[j].astype(F32)
            in1 = x0b[j] + p0 * in0
            st[2 * k + j] = jnp.where(first, in0, in1).astype(BF16)
            isend[j] = jnp.where(first, in1, in0).astype(BF16)
        copies["state"].start()

    def lin_raw():
        copies["state"].wait_recv()
        squares = jnp.zeros((tok, size), F32)
        crossed = jnp.zeros((tok, size), F32)
        for h in range(heads):
            value = rawo[h] + enter[h] * dot_nn(hb[0, h], st[h])
            rawo[h] = value
            squares += value * value
            crossed += head_of(LC, h) * ngv[h : h + 1, :] * value
        ysend[0:1, :] = jnp.sum(jnp.transpose(squares), axis=0, keepdims=True)
        ysend[1:2, :] = jnp.sum(jnp.transpose(crossed), axis=0, keepdims=True)
        for step in range(n_head - 1):
            copies["sums", step].start()

    def lin_norm():
        total = ysend[...]
        copies["all", 9].wait_recv()
        for step in range(n_head - 1):
            total += yrecv[step]
        count = heads * size * n_head
        rscale_row = lax.rsqrt(total[0:1, :] / count + NORM_EPS)
        factor_row = rscale_row * rscale_row * rscale_row * (total[1:2, :] / count)
        rscale = jnp.transpose(jnp.broadcast_to(rscale_row, (tok, tok)))
        factor = jnp.transpose(jnp.broadcast_to(factor_row, (tok, tok)))
        for h in range(heads):
            gain = ngv[h : h + 1, :]
            value = rawo[h]
            put(O_LIN, h, value * rscale * gain)
            grad = (rscale * (head_of(LC, h) * gain) - value * factor).astype(BF16)
            rgrad[h] = grad
            carried = (enter[h] * hb[0, h].astype(F32)).astype(BF16)
            pu[h] = dot_tn(carried, grad)
        copies["pulled"].start()

    def back_send():
        copies["pulled"].wait_recv()
        for j in range(half):
            own, other = pu[2 * k + j], pur[j]
            y0, y1 = jnp.where(first, own, other), jnp.where(first, other, own)
            p0, p1 = pass_rows(j)
            x0b[j] = y1
            comb[j] = y0 + p0 * y1
            rsend[j] = comb[j].astype(BF16)
            copies["r", j].start()

    def back_relay():
        for j in range(half):
            copies["r", j].wait_recv()
            both = pprod[0, pl.ds(2 * k + j, 1), :]
            qsend[j] = (comb[j] + both * rnear[j].astype(F32)).astype(BF16)
            copies["q", j].start()

    def back_get():
        for j in range(half):
            copies["q", j].wait_recv()
            p0, p1 = pass_rows(j)
            out1 = rfar[j].astype(F32)
            out0 = x0b[j] + p1 * out1
            back[2 * k + j] = jnp.where(first, out0, out1).astype(BF16)
            osend[j] = jnp.where(first, out1, out0).astype(BF16)
        copies["back"].start()

    def lin_local_grads():
        for h in range(heads):
            query, key, value, grad = hb[0, h], hb[1, h], hb[2, h], rgrad[h]
            mixed = (within[h] * dot_nt(grad, value)).astype(BF16)
            put(O_LQ, h, dot_nn(mixed, key) + enter[h] * dot_nt(grad, st[h]))
            dkp[h] = dot_tn(mixed, query)
            dvp[h] = dot_tn(attend[h], grad)

    def lin_grads():
        copies["back"].wait_recv()
        for h in range(heads):
            put(O_LK, h, dkp[h] + leave[h] * dot_nt(hb[2, h], back[h]))
            put(O_LV, h, dvp[h] + leave[h] * dot_nn(hb[1, h], back[h]))

    decays()
    closing()
    enter_kernel()
    send_closing()
    load_kv()
    send_first(0)
    load_qd()
    send_qd(0)
    send_qd(1)
    send_qd(2)
    local_lin()
    state_send()
    send_first(1)
    send_own(1)
    send_qd(3)
    local_soft()
    state_relay()
    relay(0)
    send_own(2)
    relay(1)
    send_own(3)
    qrelay(0)
    qrelay(1)
    qrelay(2)
    qrelay(3)
    state_get()
    lin_raw()
    relay_core(0)
    relay(2)
    soft(0)
    qrelay_core(0)
    qrelay_core(1)
    relay_core(1)
    relay(3)
    lin_norm()
    soft(1)
    back_send()
    qrelay_core(2)
    relay_core(2)
    lin_local_grads()
    finish(0)
    finish(1)
    soft(2)
    relay_core(3)
    qrelay_core(3)
    later_mask()
    soft_grad(0)
    back_relay()
    soft(3)
    finish(4)
    finish(5)
    soft_grad(1)
    soft_grad(2)
    back_get()
    soft_grad(3)
    lin_grads()
    finish(2)
    finish(3)
    finish(6)
    finish(7)
    for kind in range(14):
        copies["all", kind].wait_send()
    for name, _, _, _ in lin:
        copies[name].wait_send()


def write_out(*refs):
    copies = [pltpu.make_async_copy(refs[i], refs[8 + i], refs[16].at[i]) for i in range(8)]
    for copy in copies:
        copy.start()
    for copy in copies:
        copy.wait()


def shards(n_ctx, n_head, *args):
    tok, heads, size = args[0].shape
    (lq, lk, lv, ld, ng, lc, sq, sk, sv, sc, ds) = args
    flat = (tok * heads, size)
    big = [a.reshape(flat) for a in (lq, lk, lv, lc, sq, sk, sv, sc)]
    square = (heads, tok, size)
    half = (heads // 2, size, size)
    wide = (heads, SPAN + 2, 2, tok, size)
    vmem = pltpu.VMEM
    dma = pltpu.SemaphoreType.DMA
    any_spec = pl.BlockSpec(memory_space=pl.ANY)
    pair = (heads, 2, tok, size)
    scratch = [
        vmem((8,) + flat, BF16),
        vmem((8,) + flat, F32),
        vmem((3,) + square, BF16),
        vmem(wide, BF16),
        vmem((heads, tok), F32),
        vmem((heads, size), F32),
        vmem((1, tok), jnp.int32),
        vmem((tok, (SPAN + 1) * tok), F32),
        vmem((tok, (SPAN + 1) * tok), F32),
        vmem((2, tok, tok), F32),
        vmem(square, F32),
        vmem(square, F32),
        vmem(square, F32),
        vmem(wide, BF16),
        vmem((heads, SPAN + 1, 4, tok), F32),
        vmem((heads, size, size), F32),
        vmem(half, F32),
        vmem((2, 8, size), F32),
        vmem((1, 8, size), F32),
        vmem(half, F32),
        vmem(half, F32),
        vmem(half, BF16),
        vmem(half, BF16),
        vmem(half, BF16),
        vmem(half, BF16),
        vmem(half, BF16),
        vmem((heads, size, size), BF16),
        vmem((2, tok), F32),
        vmem((n_head, 2, tok), F32),
        vmem((heads, tok, tok), BF16),
        vmem(square, F32),
        vmem(square, BF16),
        vmem((heads, size, size), F32),
        vmem(half, F32),
        vmem(half, BF16),
        vmem(half, BF16),
        vmem(half, BF16),
        vmem(half, BF16),
        vmem(half, BF16),
        vmem((heads, size, size), BF16),
        vmem(square, F32),
        vmem(square, F32),
        vmem((8,) + flat, F32),
        dma((8,)),
        dma((3,)),
        dma((1,)),
        dma((4,)),
        dma((4, heads)),
        dma((4,)),
        dma((4, heads)),
        dma((1,)),
        dma((heads,)),
        dma((5,)),
        dma((5,)),
        dma((4,)),
        dma((4, heads // 2)),
        dma((1,)),
        dma((1,)),
    ]
    results = pl.pallas_call(
        functools.partial(kernel, n_ctx, n_head, heads, tok, size),
        out_shape=[vmem(flat, BF16)] * 8,
        in_specs=[any_spec] * 11,
        out_specs=[pl.BlockSpec(memory_space=pltpu.VMEM)] * 8,
        scratch_shapes=scratch,
        compiler_params=pltpu.CompilerParams(
            collective_id=0, has_side_effects=True, vmem_limit_bytes=48 * 1024 * 1024
        ),
    )(*[pltpu.with_memory_space_constraint(a, pltpu.HBM) for a in (*big, ld, ng, ds.reshape(1, tok))])
    results = pl.pallas_call(
        write_out,
        out_shape=[jax.ShapeDtypeStruct(flat, BF16)] * 8,
        in_specs=[any_spec] * 8,
        out_specs=[any_spec] * 8,
        scratch_shapes=[dma((8,))],
    )(*[pltpu.with_memory_space_constraint(r, pltpu.VMEM) for r in results])
    return tuple(r.reshape(tok, heads, size) for r in results)


def solution(mesh):
    cube = P("ctx", "head", None)
    in_specs = (
        cube, cube, cube, P("head", "ctx"), P("head", None), cube, cube, cube, cube, cube, P("ctx"),
    )
    return jax.shard_map(
        functools.partial(shards, mesh.shape["ctx"], mesh.shape["head"]),
        mesh=mesh, in_specs=in_specs, out_specs=(cube,) * 8, check_vma=False,
    )
```
